256 devices in a mesh: dp: 128 (over z, y_lo, x, core), group: 2 (over y_hi).
Axes of the slice: x: 4, y: 4 (y_hi: 2, y_lo: 2; y = y_hi * 2 + y_lo), z: 8, core: 2. Of those that a mesh axis runs over, the one named last changes fastest.
Arguments:
- atom_feats: bfloat16 [2048, 32, 512], P(('dp', 'group')), may hold values from -6 to 6
- coords: float32 [2048, 3, 32], P(('dp', 'group')), may hold values from -6 to 6
- atom_counts: int32 [2048], P(('dp', 'group')), may hold values from 8 to 32
- positives: int32 [2048], P(('dp', 'group')), may hold values from 0 to 2047, each once
- z2: bfloat16 [2048, 128], P(('dp', 'group')), may hold values from -6 to 6
- w_qkv: bfloat16 [512, 1536], replicated, may hold values from -0.25 to 0.25
- w_out: bfloat16 [512, 512], replicated, may hold values from -0.25 to 0.25
- proj: bfloat16 [512, 128], replicated, may hold values from -0.25 to 0.25
- bias_weight: float32 [128, 64], replicated, may hold values from -2 to 36
- ln_gain: float32 [512], replicated, may hold values from 0.5 to 1.5
Outputs:
- loss: float32 [], replicated
- grad_z2: float32 [2048, 128], P(('dp', 'group'))
- grad_w_qkv: float32 [512, 1536], replicated
- grad_w_out: float32 [512, 512], replicated
- grad_proj: float32 [512, 128], replicated
- grad_bias_weight: float32 [128, 64], replicated
- grad_ln_gain: float32 [512], replicated
The draws below stay inside these ranges and needn't reach their ends.
Inputs may be any that keep to these rules, and one draw needn't show every extreme that they name: positives is a permutation of the 2048 molecules.
All inputs are finite; a program needn't handle non-finite values.
Results may differ from the reference program's by a relative error of at most 0.014.
Values may be sent and summed in bfloat16 or wider, within the bound.
A program may use at most 128 MiB of HBM per device.

```python
import jax
import jax.numpy as jnp
from jax import lax

D = 512
HEADS = 64
P_SIZE = 128
KERNELS = 128
ATOMS = 32
MOL_DEV = 8
BATCH = 2048


def draw_bias_weight(key, part):
    rough = jnp.clip(0.3 * jax.random.normal(jax.random.fold_in(key, 11), (KERNELS, HEADS), jnp.float32), -2.0, 2.0)
    return rough


def plant(result, own_key, smallest, high):
    dims = result.shape
    spot = [jax.random.randint(jax.random.fold_in(own_key, axis), (), 0, dims[axis]) for axis in range(len(dims))]
    result = result.at[tuple(spot)].set(smallest)
    longest = dims.index(max(dims))
    spot[longest] = (spot[longest] + 1) % dims[longest]
    return result.at[tuple(spot)].set(high)


def block_scale(key, extent, shards, least, largest):
    def one(position, parts):
        heights = jax.random.uniform(jax.random.fold_in(jax.random.fold_in(key, 6), position), (parts,), jnp.float32, least / len(shards), largest / len(shards))
        return jnp.repeat(jnp.exp(heights), extent[position] // parts).reshape((-1,) + (1,) * (len(extent) - position - 1))

    factor_of = one(*shards[0])
    for cut in shards[1:]:
        factor_of = factor_of * one(*cut)
    return factor_of


def centred(rng, dims, scale, bound, cuts=(), dtype=jnp.bfloat16):
    values = jax.random.normal(rng, dims, jnp.float32) * scale
    if len(cuts) > 0:
        values = block_scale(rng, dims, cuts, -0.22, 0.18) * values
    return jnp.clip(values, min=-bound, max=bound).astype(dtype)


def setup_inputs(seed: int = 0) -> dict:
    key_list = jax.random.split(jax.random.key(seed), 11)
    return {
        "atom_feats": centred(key_list[0], (BATCH, ATOMS, D), 1.0, 6.0, ((0, 256),)),
        "coords": centred(key_list[1], (BATCH, 3, ATOMS), 1.5, 6.0, ((0, 256),), jnp.float32),
        "atom_counts": plant(jax.random.randint(key_list[2], (BATCH,), ATOMS // 4, ATOMS + 1), jax.random.fold_in(key_list[2], 1), ATOMS // 4, ATOMS).astype(jnp.int32),
        "positives": jax.random.permutation(key_list[3], BATCH).astype(jnp.int32),
        "z2": centred(key_list[4], (BATCH, P_SIZE), 1.0, 6.0, ((0, 256),)),
        "w_qkv": centred(key_list[5], (D, 3 * D), D ** -0.5, 0.25),
        "w_out": centred(key_list[6], (D, D), D ** -0.5, 0.25),
        "proj": centred(key_list[7], (D, P_SIZE), D ** -0.5, 0.25),
        "bias_weight": draw_bias_weight(jax.random.fold_in(key_list[10], 71), 0),
        "ln_gain": jnp.clip(1.0 + 0.1 * jax.random.normal(key_list[9], (D,), jnp.float32), 0.5, 1.5),
    }


def encode(weights_all, feats, coords, counts):
    w_qkv, w_out, proj, bias_weight, ln_gain = weights_all
    mol_count, atom_count, model_width = feats.shape
    kernels = bias_weight.shape[0]
    head_count = bias_weight.shape[1]
    head_dim = model_width // head_count
    inputs = feats.astype(jnp.float32)
    center = lax.optimization_barrier(jnp.mean(inputs, axis=-1, keepdims=True))
    spread = lax.optimization_barrier(jnp.mean((inputs - center) ** 2, axis=-1, keepdims=True))
    normed = ((inputs - center) * lax.rsqrt(spread + 1e-05) * ln_gain).astype(jnp.bfloat16)
    projected = jnp.dot(normed.reshape(mol_count * atom_count, model_width), w_qkv, preferred_element_type=jnp.float32).astype(jnp.bfloat16)
    projected = projected.reshape(mol_count, atom_count, 3, head_count, head_dim)
    query_heads = projected[:, :, 0]
    key_heads = projected[:, :, 1]
    value_heads = projected[:, :, 2]
    offsets = coords[:, :, :, None] - coords[:, :, None, :]
    distance = jnp.sqrt(lax.optimization_barrier(jnp.sum(offsets * offsets, axis=1)) + 0.25)
    centers = jnp.arange(kernels).astype(jnp.float32) * (12.0 / kernels)
    kernel_basis = jnp.exp(-((distance[..., None] - centers) / 0.5) ** 2)
    pair_bias = jnp.einsum('mijk,kh->mhij', kernel_basis, bias_weight, precision=lax.Precision.HIGHEST)
    scores = jnp.einsum('mihd,mjhd->mhij', query_heads, key_heads, preferred_element_type=jnp.float32) * head_dim ** (-0.5) + pair_bias
    is_valid = jnp.arange(atom_count)[None, :] < counts[:, None]
    scores = jnp.where(is_valid[:, None, None, :], scores, -1e+30)
    highest = lax.optimization_barrier(jnp.max(scores, axis=-1, keepdims=True))
    expo = jnp.exp(scores - highest)
    attn_weights = (expo / lax.optimization_barrier(jnp.sum(expo, axis=-1, keepdims=True))).astype(jnp.bfloat16)
    context = jnp.einsum('mhij,mjhd->mihd', attn_weights, value_heads, preferred_element_type=jnp.float32).astype(jnp.bfloat16)
    hidden = inputs + jnp.dot(context.reshape(mol_count * atom_count, model_width), w_out, preferred_element_type=jnp.float32).reshape(mol_count, atom_count, model_width)
    pooled = lax.optimization_barrier(jnp.sum(jnp.where(is_valid[..., None], hidden, 0.0), axis=1))
    return jnp.dot(pooled.astype(jnp.bfloat16), proj, preferred_element_type=jnp.float32)

def unit_rows(values):
    inverse = lax.rsqrt(lax.optimization_barrier(jnp.mean(values * values, axis=1, keepdims=True)) + 1e-06) * values.shape[1] ** (-0.5)
    return (values * inverse, inverse)

def unit_backward(values, inverse, grad):
    along = lax.optimization_barrier(jnp.sum(values * grad, axis=1, keepdims=True))
    return inverse * (grad - values * along * (inverse * inverse))

def reference(atom_feats, coords, atom_counts, positives, z2, w_qkv, w_out, proj, bias_weight, ln_gain):
    weights_all = (w_qkv, w_out, proj, bias_weight, ln_gain)
    blocks = BATCH // MOL_DEV
    feat_blocks = atom_feats.reshape(blocks, MOL_DEV, ATOMS, D)
    coord_blocks = coords.reshape(blocks, MOL_DEV, 3, ATOMS)
    count_blocks = atom_counts.reshape(blocks, MOL_DEV)

    def forward_block(entries):
        return encode(weights_all, entries[0], entries[1], entries[2])
    z3 = lax.map(forward_block, (feat_blocks, coord_blocks, count_blocks)).reshape(BATCH, P_SIZE)
    unit, inverse = unit_rows(z3)
    z3_half = unit.astype(jnp.bfloat16)
    row_blocks = z3_half.reshape(blocks, MOL_DEV, P_SIZE)
    target_blocks = positives.reshape(blocks, MOL_DEV)
    columns = jnp.arange(BATCH).astype(jnp.int32)

    def first_pass(col_total, entries):
        logits = jnp.dot(entries[0], z2.T, preferred_element_type=jnp.float32)
        expo = jnp.exp(logits)
        row_lse = jnp.log(lax.optimization_barrier(jnp.sum(expo, axis=1)))
        is_positive = entries[1][:, None] == columns[None, :]
        positive_score = lax.optimization_barrier(jnp.sum(jnp.where(is_positive, logits, 0.0), axis=1))
        return (col_total + lax.optimization_barrier(jnp.sum(expo, axis=0)), (row_lse, jnp.sum(0.5 * row_lse - positive_score)))
    col_total, (lse_blocks, row_terms) = lax.scan(first_pass, jnp.zeros((BATCH,), jnp.float32), (row_blocks, target_blocks))
    col_lse = jnp.log(col_total)
    loss = (jnp.sum(row_terms) + 0.5 * jnp.sum(col_lse)) / BATCH

    def second_pass(grad_cols, entries):
        logits = jnp.dot(entries[0], z2.T, preferred_element_type=jnp.float32)
        is_positive = entries[1][:, None] == columns[None, :]
        slope = (0.5 * jnp.exp(logits - entries[2][:, None]) + 0.5 * jnp.exp(logits - col_lse[None, :]) - is_positive.astype(jnp.float32)).astype(jnp.bfloat16)
        grad_rows = jnp.dot(slope, z2, preferred_element_type=jnp.float32)
        grad_cols = grad_cols + lax.dot_general(slope, entries[0], (((0,), (0,)), ((), ())), preferred_element_type=jnp.float32)
        return (grad_cols, grad_rows)
    grad_z2, unit_grads = lax.scan(second_pass, jnp.zeros((BATCH, P_SIZE), jnp.float32), (row_blocks, target_blocks, lse_blocks))
    grad_z3 = unit_backward(z3, inverse, unit_grads.reshape(BATCH, P_SIZE))
    grad_blocks = grad_z3.reshape(blocks, MOL_DEV, P_SIZE)

    def accumulate(running, entries):

        def local_encode(params_in):
            return encode(params_in, entries[0], entries[1], entries[2])
        unused, pullback = jax.vjp(local_encode, weights_all)
        pieces = pullback(entries[3])[0]
        return (tuple((a + b.astype(jnp.float32) for a, b in zip(running, pieces))), None)
    start_sums = tuple((jnp.zeros(w.shape, jnp.float32) for w in weights_all))
    sums, unused = lax.scan(accumulate, start_sums, (feat_blocks, coord_blocks, count_blocks, grad_blocks))
    return (loss, grad_z2, sums[0], sums[1], sums[2], sums[3], sums[4])
```

```python
import functools

import jax
import jax.numpy as jnp
from jax import lax
from jax.experimental import pallas as pl
from jax.experimental.pallas import tpu as pltpu
from jax.sharding import PartitionSpec as P

MESH = pl.DeviceIdType.MESH
F32 = jnp.float32
BF = jnp.bfloat16

MOLS = 8
PAIRS = 4
ATOMS = 32
WIDTH = 512
HEADS = 64
HEAD_DIM = 8
KERNELS = 128
LANES = 128
WIDE = HEAD_DIM * LANES
BATCH = 2048
SIDE = 16
DEPTH = 8
PAYLOAD = 2048

Z2, POS, Z3, ROWS, COLS, UNIT, GZ2, CORE, PLANE, RING, RING_OUT, PLANE_OUT, CORE_OUT = range(13)


def mm(a, b):
    return lax.dot_general(a, b, (((1,), (0,)), ((), ())), preferred_element_type=F32)


def mm_t(a, b):
    return lax.dot_general(a, b, (((1,), (1,)), ((), ())), preferred_element_type=F32)


def tmm(a, b):
    return lax.dot_general(a, b, (((0,), (0,)), ((), ())), preferred_element_type=F32)


def halves(values):
    high = values.astype(BF)
    return high, (values - high.astype(F32)).astype(BF)


def stacked(values):
    high = values.astype(BF).astype(F32)
    return jnp.concatenate([high, values - high], axis=0).astype(BF)


def two_part(values, weights, product):
    rows = values.shape[0]
    both = product(stacked(values), weights)
    return both[:rows] + both[rows:]


def lane_is_odd(shape):
    return (lax.broadcasted_iota(jnp.int32, shape, len(shape) - 1) & 64) != 0


def device_of(place):
    return (place // 2, place % 2)


def remote(src, dst, sems, kind, slot, place):
    return pltpu.make_async_remote_copy(
        src_ref=src,
        dst_ref=dst,
        send_sem=sems[0].at[kind, slot],
        recv_sem=sems[1].at[kind, slot],
        device_id=device_of(place),
        device_id_type=MESH,
    )


def forward(feats, coords, counts, wqkv, wout, proj, bias_weight, gain, s):
    x = feats[...].astype(F32)
    mean = jnp.mean(x, axis=-1, keepdims=True)
    centred = x - mean
    var = jnp.mean(centred * centred, axis=-1, keepdims=True)
    xhat = centred * lax.rsqrt(var + 1e-05)
    s.xhat[...] = xhat
    normed = (xhat * gain[...]).astype(BF)
    s.normed[...] = normed
    for m in range(MOLS):
        valid = lax.broadcasted_iota(jnp.int32, (ATOMS, WIDTH), 0) < counts[m]
        s.xsum[m : m + 1, :] = jnp.sum(
            jnp.where(valid, x[m * ATOMS : (m + 1) * ATOMS], 0.0), axis=0, keepdims=True
        )

    row = lax.broadcasted_iota(jnp.int32, (WIDTH, WIDE), 0)
    col = lax.broadcasted_iota(jnp.int32, (WIDTH, WIDE), 1)
    placed = ((row >> 3) == (col & 63)) & ((row & 7) == (col >> 7))
    s.perm[...] = jnp.where(placed, 1.0, 0.0).astype(BF)

    odd = lane_is_odd((ATOMS, WIDE))
    for part, (target, scale) in enumerate(((s.q, HEAD_DIM ** (-0.5)), (s.k, 1.0), (s.v, 1.0))):
        projected = mm(normed, wqkv[:, part * WIDTH : (part + 1) * WIDTH]).astype(BF)
        spread = mm(projected, s.perm[...])
        for p in range(PAIRS):
            low = spread[(2 * p) * ATOMS : (2 * p + 1) * ATOMS]
            high = spread[(2 * p + 1) * ATOMS : (2 * p + 2) * ATOMS]
            merged = jnp.where(odd, high, low)
            target[p] = merged * scale if scale != 1.0 else merged

    atom = lax.broadcasted_iota(jnp.int32, (ATOMS, ATOMS * ATOMS), 0)
    pair = lax.broadcasted_iota(jnp.int32, (ATOMS, ATOMS * ATOMS), 1)
    select = (
        jnp.where(atom == (pair & 31), 1.0, 0.0) - jnp.where(atom == (pair >> 5), 1.0, 0.0)
    ).astype(BF)
    squared = jnp.zeros((MOLS, ATOMS * ATOMS), F32)
    for c in range(3):
        values = coords[c]
        first = values.astype(BF).astype(F32)
        second = (values - first).astype(BF).astype(F32)
        third = values - first - second
        three = mm(jnp.concatenate([first, second, third], axis=0).astype(BF), select)
        offset = three[:MOLS] + three[MOLS : 2 * MOLS] + three[2 * MOLS :]
        squared = squared + offset * offset
    distance = jnp.sqrt(squared + 0.25)
    for m in range(MOLS):
        s.distance[m] = distance[m : m + 1]

    wide = jnp.concatenate([bias_weight[...], bias_weight[...]], axis=1)
    turned = wide.T
    upper = lax.broadcasted_iota(jnp.int32, (LANES, KERNELS), 0) < HEADS
    blocks = jnp.concatenate([jnp.where(upper, turned, 0.0), jnp.where(upper, 0.0, turned)], axis=1)
    s.bias_lhs[...] = stacked(blocks)

    centers = lax.broadcasted_iota(jnp.int32, (KERNELS, 2 * LANES), 0).astype(F32) * (12.0 / KERNELS)

    def one_pair(p, carry):
        count = jnp.where(lane_is_odd((1, LANES)), counts[2 * p + 1], counts[2 * p])
        for block in range(4):
            at = pl.ds(block * 256, 256)
            basis = []
            for parity in range(2):
                away = (s.distance[2 * p + parity, :, at] - centers) * 2.0
                basis.append(jnp.exp(-(away * away)))
            high, low = halves(jnp.concatenate(basis, axis=0))
            s.basis[p, :, at] = high
            both = mm(s.bias_lhs[...], high)
            bias = both[:LANES] + both[LANES:] + mm(s.bias_lhs[:LANES, :], low)
            s.attn[p, at, :] = bias.T
        top = jnp.full((ATOMS, LANES), -1e30, F32)
        for j in range(ATOMS):
            at = pl.ds(j * ATOMS, ATOMS)
            score = s.attn[p, at, :]
            for d in range(HEAD_DIM):
                lanes = pl.ds(d * LANES, LANES)
                score = score + s.q[p, :, lanes] * s.k[p, j : j + 1, lanes]
            score = jnp.where(j < count, score, -1e30)
            s.attn[p, at, :] = score
            top = jnp.maximum(top, score)
        total = jnp.zeros((ATOMS, LANES), F32)
        for j in range(ATOMS):
            at = pl.ds(j * ATOMS, ATOMS)
            expo = jnp.exp(s.attn[p, at, :] - top)
            s.attn[p, at, :] = expo
            total = total + expo
        real = lax.broadcasted_iota(jnp.int32, (ATOMS, LANES), 0) < count
        share = jnp.where(real, 1.0 / total, 0.0)
        for j in range(ATOMS):
            at = pl.ds(j * ATOMS, ATOMS)
            weight = s.attn[p, at, :] * share
            s.attn[p, at, :] = weight
            s.column[p, j : j + 1, :] = jnp.sum(weight, axis=0, keepdims=True)
        odd_row = lane_is_odd((1, LANES))
        for d in range(HEAD_DIM):
            lanes = pl.ds(d * LANES, LANES)
            context = jnp.sum(s.column[p] * s.v[p, :, lanes], axis=0, keepdims=True)
            s.context[2 * p, :, lanes] = jnp.where(odd_row, 0.0, context)
            s.context[2 * p + 1, :, lanes] = jnp.where(odd_row, context, 0.0)
        return carry

    lax.fori_loop(0, PAIRS, one_pair, 0)
    context = jnp.concatenate([s.context[m] for m in range(MOLS)], axis=0)
    context = two_part(context, s.perm[...], mm_t)
    s.ctx_sum[...] = context
    pooled = (s.xsum[...] + two_part(context, wout[...], mm)).astype(BF)
    s.pooled[...] = pooled.astype(F32)
    return mm(pooled, proj[...])


def backward(grad_z3, wqkv, wout, proj, s):
    cs_high, cs_low = halves(s.ctx_sum[...])
    g_high, g_low = halves(grad_z3)
    f = lambda v: v.astype(F32)
    left = jnp.concatenate([f(cs_high), f(cs_low), f(cs_high)], axis=0).astype(BF)
    right = jnp.concatenate([f(g_high), f(g_high), f(g_low)], axis=0).astype(BF)
    s.payload[:, 1536:1664] = tmm(left, right).astype(BF)
    left = jnp.concatenate([s.pooled[...], s.pooled[...]], axis=0).astype(BF)
    right = jnp.concatenate([f(g_high), f(g_low)], axis=0).astype(BF)
    s.payload[:, 1664:1792] = tmm(left, right).astype(BF)

    grad_pooled = two_part(grad_z3, proj[...], mm_t)
    grad_ctx = two_part(grad_pooled, wout[...], mm_t)
    spread = two_part(grad_ctx, s.perm[...], mm)
    for m in range(MOLS):
        s.context[m] = spread[m : m + 1]

    scale = HEAD_DIM ** (-0.5)
    odd_row = lane_is_odd((1, LANES))

    def one_pair(p, bias_sum):
        along = jnp.zeros((ATOMS, LANES), F32)
        for d in range(HEAD_DIM):
            lanes = pl.ds(d * LANES, LANES)
            grad = jnp.where(
                odd_row, s.context[2 * p + 1, :, lanes], s.context[2 * p, :, lanes]
            )
            along = along + grad * s.v[p, :, lanes]
            s.dv[p, :, lanes] = (s.column[p] * grad).astype(BF)
        s.along[...] = along
        mean = jnp.zeros((ATOMS, LANES), F32)
        for j in range(ATOMS):
            mean = mean + s.attn[p, pl.ds(j * ATOMS, ATOMS), :] * s.along[j : j + 1, :]
        for d in range(HEAD_DIM):
            s.dq[:, pl.ds(d * LANES, LANES)] = jnp.zeros((ATOMS, LANES), F32)
        for half in range(2):
            ds_range = range(4 * half, 4 * half + 4)
            sums = [jnp.zeros((ATOMS, LANES), F32) for d in ds_range]
            for j in range(ATOMS):
                at = pl.ds(j * ATOMS, ATOMS)
                if half == 0:
                    slope = s.attn[p, at, :] * (s.along[j : j + 1, :] - mean)
                    s.attn[p, at, :] = slope
                else:
                    slope = s.attn[p, at, :]
                for n, d in enumerate(ds_range):
                    lanes = pl.ds(d * LANES, LANES)
                    sums[n] = sums[n] + slope * s.k[p, j : j + 1, lanes]
                    s.dk[j : j + 1, lanes] = jnp.sum(slope * s.q[p, :, lanes], axis=0, keepdims=True)
            for n, d in enumerate(ds_range):
                s.dq[:, pl.ds(d * LANES, LANES)] = sums[n] * scale
        s.dqs[p] = s.dq[...].astype(BF)
        s.dks[p] = s.dk[...].astype(BF)
        return bias_sum + mm(s.basis[p], s.attn[p].astype(BF))

    bias_sum = lax.fori_loop(0, PAIRS, one_pair, jnp.zeros((2 * KERNELS, LANES), F32))
    odd = lane_is_odd((KERNELS, LANES))
    folded = jnp.where(odd, bias_sum[KERNELS:], bias_sum[:KERNELS])
    folded = folded + pltpu.roll(folded, 64, 1)
    s.small[...] = jnp.zeros((WIDTH, LANES), F32)
    s.small[0:64, :] = jnp.where(lane_is_odd((64, LANES)), folded[64:], folded[:64])

    odd = lane_is_odd((ATOMS, WIDE))
    zero = jnp.zeros((ATOMS, WIDE), BF)
    for part, source in enumerate((s.dqs, s.dks, s.dv)):
        pieces = []
        for m in range(MOLS):
            value = source[m // 2]
            pieces.append(jnp.where(odd, value, zero) if m % 2 else jnp.where(odd, zero, value))
        s.dproj[:, part * WIDTH : (part + 1) * WIDTH] = mm_t(
            jnp.concatenate(pieces, axis=0), s.perm[...]
        ).astype(BF)
    for part in range(3):
        at = pl.ds(part * WIDTH, WIDTH)
        s.payload[:, at] = tmm(s.normed[...], s.dproj[:, at]).astype(BF)
    grad_normed = mm_t(s.dproj[...], wqkv[...])
    grad_gain = jnp.sum(grad_normed * s.xhat[...], axis=0, keepdims=True)
    for n in range(4):
        s.small[64 + n : 65 + n, :] = grad_gain[:, n * LANES : (n + 1) * LANES]


def fused(
    counts,
    positives,
    feats,
    coords,
    z2,
    wqkv,
    wout,
    proj,
    bias_weight,
    gain,
    summed,
    grad_z2,
    *scratch,
):
    s = Scratch(scratch)
    sems = (s.send, s.recv)
    me = lax.axis_index("dp") * 2 + lax.axis_index("group")
    row_group, col_group = me // SIDE, me % SIDE
    core = (me // 2) % 2
    sibling = me + 2 - 4 * core
    plane = ((me // 16) % 2) * 8 + ((me // 4) % 4) * 2 + me % 2
    ring = me // 32

    def along_row(n):
        return row_group * SIDE + n

    def along_col(n):
        return n * SIDE + col_group

    def in_plane(n):
        return ring * 32 + (n // 8) * 16 + ((n // 2) % 4) * 4 + core * 2 + n % 2

    def in_ring(n):
        return n * 32 + me % 32

    barrier = pltpu.get_barrier_semaphore()

    def signal(place):
        pl.semaphore_signal(barrier, inc=1, device_id=device_of(place), device_id_type=MESH)

    def greet(o, carry):
        signal(along_row((col_group + o) % SIDE))
        signal(along_col((row_group + o) % SIDE))
        signal(in_plane((plane + o) % SIDE))
        return carry

    lax.fori_loop(1, SIDE, greet, 0)

    def greet_ring(o, carry):
        signal(in_ring((ring + o) % DEPTH))
        return carry

    lax.fori_loop(1, DEPTH, greet_ring, 0)
    signal(sibling)
    pl.semaphore_wait(barrier, 3 * (SIDE - 1) + (DEPTH - 1) + 1)

    def slot(n):
        return pl.ds(n * 8, 8)

    def each(count, body):
        def step(o, carry):
            body(o)
            return carry

        lax.fori_loop(1, count, step, 0)

    s.z2[slot(row_group), :] = z2[...].astype(F32)
    targets = jnp.zeros((8, LANES), jnp.int32)
    sub = lax.broadcasted_iota(jnp.int32, (8, LANES), 0)
    for n in range(8):
        targets = jnp.where(sub == n, positives[n], targets)
    s.pos[slot(col_group), :] = targets

    def z2_copy(o):
        mine = s.z2.at[slot(row_group), :]
        return remote(mine, mine, sems, Z2, o, along_col((row_group + o) % SIDE))

    def pos_copy(o):
        mine = s.pos.at[slot(col_group), :]
        return remote(mine, mine, sems, POS, o, along_row((col_group + o) % SIDE))

    def z3_copy(o):
        mine = s.z3.at[slot(col_group), :]
        return remote(mine, mine, sems, Z3, o, along_row((col_group + o) % SIDE))

    def rows_copy(o):
        mine = s.rows.at[col_group]
        return remote(mine, mine, sems, ROWS, o, along_row((col_group + o) % SIDE))

    def cols_copy(o):
        mine = s.cols.at[row_group]
        return remote(mine, mine, sems, COLS, o, along_col((row_group + o) % SIDE))

    def unit_copy(o):
        peer = (col_group + o) % SIDE
        return remote(s.unit.at[peer], s.unit_in.at[col_group], sems, UNIT, o, along_row(peer))

    def gz2_copy(o):
        peer = (row_group + o) % SIDE
        return remote(s.gz2.at[peer], s.gz2_in.at[row_group], sems, GZ2, o, along_col(peer))

    each(SIDE, lambda o: z2_copy(o).start())
    each(SIDE, lambda o: pos_copy(o).start())

    z3 = forward(feats, coords, counts, wqkv, wout, proj, bias_weight, gain, s)
    inverse = lax.rsqrt(jnp.mean(z3 * z3, axis=1, keepdims=True) + 1e-06) * LANES ** (-0.5)
    s.z3[slot(col_group), :] = (z3 * inverse).astype(BF).astype(F32)
    each(SIDE, lambda o: z3_copy(o).start())
    each(SIDE, lambda o: z2_copy(o).wait())
    each(SIDE, lambda o: pos_copy(o).wait())
    each(SIDE, lambda o: z3_copy(o).wait())

    z3_all = s.z3[...].astype(BF)
    z2_all = s.z2[...].astype(BF)
    logits = mm_t(z3_all, z2_all)
    expo = jnp.exp(logits)
    expo_t = jnp.exp(mm_t(z2_all, z3_all))
    s.rows[col_group] = jnp.broadcast_to(jnp.sum(expo_t, axis=0, keepdims=True), (8, LANES))
    s.cols[row_group] = jnp.broadcast_to(jnp.sum(expo, axis=0, keepdims=True), (8, LANES))
    each(SIDE, lambda o: rows_copy(o).start())
    each(SIDE, lambda o: cols_copy(o).start())
    lane = lax.broadcasted_iota(jnp.int32, (LANES, LANES), 1)
    column_id = (lane >> 3) * LANES + col_group * 8 + (lane & 7)
    hit = s.pos[...] == column_id
    score = jnp.sum(jnp.where(hit, logits, 0.0), axis=0, keepdims=True)
    each(SIDE, lambda o: rows_copy(o).wait())
    each(SIDE, lambda o: cols_copy(o).wait())
    row_sum = s.rows[0]
    col_sum = s.cols[0]
    for n in range(1, SIDE):
        row_sum = row_sum + s.rows[n]
        col_sum = col_sum + s.cols[n]
    row_half = jnp.broadcast_to(0.5 / row_sum[0:1], (LANES, LANES)).T
    slope = expo * (row_half + 0.5 / col_sum[0:1]) - jnp.where(hit, 1.0, 0.0)
    unit = mm(slope.astype(BF), z2_all)
    for n in range(SIDE):
        s.unit[n] = unit[n * 8 : (n + 1) * 8]
    s.unit_in[col_group] = s.unit[col_group]
    each(SIDE, lambda o: unit_copy(o).start())
    grad_cols = tmm(slope.astype(BF), z3_all)
    for n in range(SIDE):
        s.gz2[n] = grad_cols[n * 8 : (n + 1) * 8]
    s.gz2_in[row_group] = s.gz2[row_group]
    each(SIDE, lambda o: gz2_copy(o).start())
    one_lane = lax.broadcasted_iota(jnp.int32, (1, LANES), 1)
    row_term = jnp.where((one_lane >> 3) == col_group, 0.5 * jnp.log(row_sum[0:1]), 0.0)
    col_term = jnp.where((one_lane >> 3) == row_group, 0.5 * jnp.log(col_sum[0:1]), 0.0)
    loss_terms = row_term + col_term - score

    each(SIDE, lambda o: unit_copy(o).wait())
    grad_unit = s.unit_in[0]
    for n in range(1, SIDE):
        grad_unit = grad_unit + s.unit_in[n]
    dot = jnp.sum(z3 * grad_unit, axis=1, keepdims=True)
    grad_z3 = inverse * (grad_unit - z3 * dot * (inverse * inverse))

    backward(grad_z3, wqkv, wout, proj, s)
    s.small[68:69, :] = loss_terms
    s.payload[:, 1792:1920] = s.small[...].astype(BF)
    s.payload[:, 1920:2048] = jnp.zeros((WIDTH, LANES), BF)

    def piece(half, n):
        return pl.ds(half * 256 + n * 16, 16)

    def core_copy(o):
        n = (plane + o) % SIDE
        return remote(
            s.payload.at[piece(1 - core, n), :], s.core_in.at[n], sems, CORE, o, sibling
        )

    def plane_copy(o):
        n = (plane + o) % SIDE
        return remote(s.plane_out.at[n], s.plane_in.at[plane], sems, PLANE, o, in_plane(n))

    def ring_copy(o):
        n = (ring + o) % DEPTH
        return remote(
            s.ring_out.at[:, pl.ds(pl.multiple_of(n * 256, 256), 256)],
            s.ring_in.at[ring],
            sems,
            RING,
            o,
            in_ring(n),
        )

    def ring_share(o):
        mine = summed.at[piece(core, plane), pl.ds(pl.multiple_of(ring * 256, 256), 256)]
        return remote(mine, mine, sems, RING_OUT, o, in_ring((ring + o) % DEPTH))

    def plane_share(o):
        mine = summed.at[piece(core, plane), :]
        return remote(mine, mine, sems, PLANE_OUT, o, in_plane((plane + o) % SIDE))

    def core_share(o):
        mine = summed.at[piece(core, (plane - o + SIDE) % SIDE), :]
        return remote(mine, mine, sems, CORE_OUT, o, sibling)

    each(SIDE + 1, lambda o: core_copy(o).start())

    def core_sum(o):
        core_copy(o).wait_recv()
        n = (plane + o) % SIDE
        return (
            s.payload[piece(core, n), :].astype(F32) + s.core_in[n].astype(F32)
        ).astype(BF)

    def pass_on(o):
        s.plane_out[(plane + o) % SIDE] = core_sum(o)
        plane_copy(o).start()

    each(SIDE, pass_on)
    s.plane_in[plane] = core_sum(SIDE)
    each(SIDE, lambda o: plane_copy(o).wait())
    total = s.plane_in[0].astype(F32)
    for n in range(1, SIDE):
        total = total + s.plane_in[n].astype(F32)
    s.ring_out[...] = total.astype(BF)
    each(DEPTH, lambda o: ring_copy(o).start())
    s.ring_in[ring] = s.ring_out[:, pl.ds(pl.multiple_of(ring * 256, 256), 256)]
    each(DEPTH, lambda o: ring_copy(o).wait())
    total = s.ring_in[0].astype(F32)
    for n in range(1, DEPTH):
        total = total + s.ring_in[n].astype(F32)
    summed[piece(core, plane), pl.ds(pl.multiple_of(ring * 256, 256), 256)] = total.astype(BF)
    each(DEPTH, lambda o: ring_share(o).start())
    each(DEPTH, lambda o: ring_share(o).wait())
    each(SIDE, lambda o: plane_share(o).start())
    core_share(0).start()

    def forward_piece(o):
        plane_share(o).wait_recv()
        core_share(o).start()

    each(SIDE, forward_piece)
    each(SIDE, lambda o: gz2_copy(o).wait())
    total = s.gz2_in[0]
    for n in range(1, SIDE):
        total = total + s.gz2_in[n]
    grad_z2[...] = total
    each(SIDE + 1, lambda o: core_copy(o).wait_send())
    each(SIDE, lambda o: plane_share(o).wait_send())
    core_share(0).wait()
    each(SIDE, lambda o: core_share(o).wait())


SHAPES = {
    "xhat": ((256, WIDTH), F32),
    "normed": ((256, WIDTH), BF),
    "xsum": ((MOLS, WIDTH), F32),
    "perm": ((WIDTH, WIDE), BF),
    "q": ((PAIRS, ATOMS, WIDE), F32),
    "k": ((PAIRS, ATOMS, WIDE), F32),
    "v": ((PAIRS, ATOMS, WIDE), F32),
    "distance": ((MOLS, 1, ATOMS * ATOMS), F32),
    "bias_lhs": ((2 * LANES, 2 * KERNELS), BF),
    "basis": ((PAIRS, 2 * KERNELS, ATOMS * ATOMS), BF),
    "attn": ((PAIRS, ATOMS * ATOMS, LANES), F32),
    "column": ((PAIRS, ATOMS, LANES), F32),
    "context": ((MOLS, 1, WIDE), F32),
    "ctx_sum": ((MOLS, WIDTH), F32),
    "pooled": ((MOLS, WIDTH), F32),
    "along": ((ATOMS, LANES), F32),
    "dq": ((ATOMS, WIDE), F32),
    "dk": ((ATOMS, WIDE), F32),
    "dqs": ((PAIRS, ATOMS, WIDE), BF),
    "dks": ((PAIRS, ATOMS, WIDE), BF),
    "dv": ((PAIRS, ATOMS, WIDE), BF),
    "dproj": ((256, 3 * WIDTH), BF),
    "small": ((WIDTH, LANES), F32),
    "payload": ((WIDTH, PAYLOAD), BF),
    "z2": ((LANES, LANES), F32),
    "pos": ((LANES, LANES), jnp.int32),
    "z3": ((LANES, LANES), F32),
    "rows": ((SIDE, 8, LANES), F32),
    "cols": ((SIDE, 8, LANES), F32),
    "unit": ((SIDE, 8, LANES), F32),
    "unit_in": ((SIDE, 8, LANES), F32),
    "gz2": ((SIDE, 8, LANES), F32),
    "gz2_in": ((SIDE, 8, LANES), F32),
    "core_in": ((SIDE, 16, PAYLOAD), BF),
    "plane_out": ((SIDE, 16, PAYLOAD), BF),
    "plane_in": ((SIDE, 16, PAYLOAD), BF),
    "ring_out": ((16, PAYLOAD), BF),
    "ring_in": ((DEPTH, 16, 256), BF),
}


class Scratch:
    def __init__(self, refs):
        for name, ref in zip(list(SHAPES) + ["send", "recv"], refs):
            setattr(self, name, ref)


def unpack(summed, proj, g_qkv, g_out, g_proj, small):
    g_qkv[...] = summed[:, 0:1536].astype(F32)
    g_out[...] = mm_t(summed[:, 1536:1664], proj[...])
    g_proj[...] = summed[:, 1664:1792].astype(F32)
    small[...] = summed[0:80, 1792:1920].astype(F32)


def on_device(
    atom_feats, coords, atom_counts, positives, z2, w_qkv, w_out, proj, bias_weight, ln_gain
):
    vmem = pl.BlockSpec(memory_space=pltpu.VMEM)
    smem = pl.BlockSpec(memory_space=pltpu.SMEM)
    summed, grad_z2 = pl.pallas_call(
        fused,
        out_shape=(
            jax.ShapeDtypeStruct((WIDTH, PAYLOAD), BF),
            jax.ShapeDtypeStruct((8, LANES), F32),
        ),
        in_specs=[smem, smem] + [vmem] * 8,
        out_specs=(vmem, vmem),
        scratch_shapes=[pltpu.VMEM(*shape) for shape in SHAPES.values()]
        + [pltpu.SemaphoreType.DMA((13, SIDE + 1))] * 2,
        compiler_params=pltpu.CompilerParams(
            collective_id=0, has_side_effects=True, vmem_limit_bytes=56 * 1024 * 1024
        ),
        name="pretrain_step",
    )(
        atom_counts,
        positives,
        atom_feats.reshape(256, WIDTH),
        coords.transpose(1, 0, 2),
        z2,
        w_qkv,
        w_out,
        proj,
        bias_weight,
        ln_gain.reshape(1, WIDTH),
    )
    g_qkv, g_out, g_proj, small = pl.pallas_call(
        unpack,
        out_shape=(
            jax.ShapeDtypeStruct((WIDTH, 3 * WIDTH), F32),
            jax.ShapeDtypeStruct((WIDTH, WIDTH), F32),
            jax.ShapeDtypeStruct((WIDTH, LANES), F32),
            jax.ShapeDtypeStruct((80, LANES), F32),
        ),
        in_specs=[vmem, vmem],
        out_specs=(vmem,) * 4,
        compiler_params=pltpu.CompilerParams(vmem_limit_bytes=56 * 1024 * 1024),
        name="unpack",
    )(summed, proj)
    g_bias = jnp.concatenate([small[0:64, 0:64], small[0:64, 64:128]], axis=0)
    g_gain = small[64:68].reshape(WIDTH)
    loss = jnp.sum(small[68]) / BATCH
    return (loss, grad_z2, g_qkv, g_out, g_proj, g_bias, g_gain)


def solution(mesh):
    return jax.shard_map(
        on_device,
        mesh=mesh,
        in_specs=(
            P(("dp", "group"), None, None),
            P(("dp", "group"), None, None),
            P(("dp", "group")),
            P(("dp", "group")),
            P(("dp", "group"), None),
            P(),
            P(),
            P(),
            P(),
            P(),
        ),
        out_specs=(P(), P(("dp", "group"), None), P(), P(), P(), P(), P()),
        check_vma=False,
    )
```

```python
import functools

import jax
import jax.numpy as jnp
from jax import lax
from jax.experimental import pallas as pl
from jax.experimental.pallas import tpu as pltpu
from jax.sharding import PartitionSpec as P

MESH = pl.DeviceIdType.MESH
F32 = jnp.float32
BF = jnp.bfloat16

MOLS = 8
PAIRS = 4
ATOMS = 32
WIDTH = 512
HEADS = 64
HEAD_DIM = 8
KERNELS = 128
LANES = 128
WIDE = HEAD_DIM * LANES
BATCH = 2048
SIDE = 16
DEPTH = 8

VALUE, CTX, HEAD, QUERY, KEY, SMALL, PAYLOAD = 0, 512, 640, 768, 1280, 1792, 1920
CHUNKS = (((0, 384), (384, 768)), ((768, 1152), (1152, 1536)), ((1536, 1792), (1792, 1920)))

Z2, POS, Z3, ROWS, COLS, UNIT, GZ2 = range(7)
FIRST, SECOND, RING, SHARE_SECOND, SHARE_FIRST, CORE_OUT = (7 + 6 * n for n in range(6))
CORE = 43
KINDS = CORE + 3


def mm(a, b):
    return lax.dot_general(a, b, (((1,), (0,)), ((), ())), preferred_element_type=F32)


def mm_t(a, b):
    return lax.dot_general(a, b, (((1,), (1,)), ((), ())), preferred_element_type=F32)


def tmm(a, b):
    return lax.dot_general(a, b, (((0,), (0,)), ((), ())), preferred_element_type=F32)


def halves(values):
    high = values.astype(BF)
    return high, (values - high.astype(F32)).astype(BF)


def stacked(values):
    high = values.astype(BF).astype(F32)
    return jnp.concatenate([high, values - high], axis=0).astype(BF)


def two_part(values, weights, product):
    rows = values.shape[0]
    both = product(stacked(values), weights)
    return both[:rows] + both[rows:]


def lane_is_odd(shape):
    return (lax.broadcasted_iota(jnp.int32, shape, len(shape) - 1) & 64) != 0


def remote(src, dst, sems, kind, device):
    return pltpu.make_async_remote_copy(
        src_ref=src,
        dst_ref=dst,
        send_sem=sems[0].at[kind],
        recv_sem=sems[1].at[kind],
        device_id=device,
        device_id_type=MESH,
    )


def subsets(flips, start):
    places = [start]
    for flip in flips:
        places = places + [tuple(p + f for p, f in zip(place, flip)) for place in places]
    return places


def normalize(feats, counts, gain, s):
    x = feats[...].astype(F32)
    mean = jnp.mean(x, axis=-1, keepdims=True)
    centred = x - mean
    var = jnp.mean(centred * centred, axis=-1, keepdims=True)
    xhat = centred * lax.rsqrt(var + 1e-05)
    s.xhat[...] = xhat
    normed = (xhat * gain[...]).astype(BF)
    s.normed[...] = normed
    for m in range(MOLS):
        valid = lax.broadcasted_iota(jnp.int32, (ATOMS, WIDTH), 0) < counts[m]
        s.xsum[m : m + 1, :] = jnp.sum(
            jnp.where(valid, x[m * ATOMS : (m + 1) * ATOMS], 0.0), axis=0, keepdims=True
        )


def make_perm(s):
    row = lax.broadcasted_iota(jnp.int32, (WIDTH, WIDE), 0)
    col = lax.broadcasted_iota(jnp.int32, (WIDTH, WIDE), 1)
    placed = ((row >> 3) == (col & 63)) & ((row & 7) == (col >> 7))
    s.perm[...] = jnp.where(placed, 1.0, 0.0).astype(BF)


def project(wqkv, s):
    normed = s.normed[...]
    odd = lane_is_odd((ATOMS, WIDE))
    for part, (target, scale) in enumerate(((s.q, HEAD_DIM ** (-0.5)), (s.k, 1.0), (s.v, 1.0))):
        projected = mm(normed, wqkv[:, part * WIDTH : (part + 1) * WIDTH]).astype(BF)
        spread = mm(projected, s.perm[...])
        for p in range(PAIRS):
            low = spread[(2 * p) * ATOMS : (2 * p + 1) * ATOMS]
            high = spread[(2 * p + 1) * ATOMS : (2 * p + 2) * ATOMS]
            merged = jnp.where(odd, high, low)
            target[p] = merged * scale if scale != 1.0 else merged


def distances(coords, s):
    atom = lax.broadcasted_iota(jnp.int32, (ATOMS, ATOMS * ATOMS), 0)
    pair = lax.broadcasted_iota(jnp.int32, (ATOMS, ATOMS * ATOMS), 1)
    select = (
        jnp.where(atom == (pair & 31), 1.0, 0.0) - jnp.where(atom == (pair >> 5), 1.0, 0.0)
    ).astype(BF)
    squared = jnp.zeros((MOLS, ATOMS * ATOMS), F32)
    for c in range(3):
        values = coords[c]
        first = values.astype(BF).astype(F32)
        second = (values - first).astype(BF).astype(F32)
        third = values - first - second
        three = mm(jnp.concatenate([first, second, third], axis=0).astype(BF), select)
        offset = three[:MOLS] + three[MOLS : 2 * MOLS] + three[2 * MOLS :]
        squared = squared + offset * offset
    distance = jnp.sqrt(squared + 0.25)
    for m in range(MOLS):
        s.distance[m] = distance[m : m + 1]


def bias_matrix(bias_t, s):
    turned = jnp.concatenate([bias_t[...], bias_t[...]], axis=0)
    upper = lax.broadcasted_iota(jnp.int32, (LANES, KERNELS), 0) < HEADS
    blocks = jnp.concatenate([jnp.where(upper, turned, 0.0), jnp.where(upper, 0.0, turned)], axis=1)
    s.bias_lhs[...] = stacked(blocks)


def pair_biases(s):
    centers = lax.broadcasted_iota(jnp.int32, (KERNELS, 2 * LANES), 0).astype(F32) * (12.0 / KERNELS)

    def one_pair(p, carry):
        for block in range(4):
            at = pl.ds(block * 256, 256)
            basis = []
            for parity in range(2):
                away = (s.distance[2 * p + parity, :, at] - centers) * 2.0
                basis.append(jnp.exp(-(away * away)))
            high, low = halves(jnp.concatenate(basis, axis=0))
            s.basis[p, :, at] = high
            both = mm(s.bias_lhs[...], high)
            bias = both[:LANES] + both[LANES:] + mm(s.bias_lhs[:LANES, :], low)
            s.attn[p, at, :] = bias.T
        return carry

    lax.fori_loop(0, PAIRS, one_pair, 0)


def attend(counts, s):
    def one_pair(p, carry):
        count = jnp.where(lane_is_odd((1, LANES)), counts[2 * p + 1], counts[2 * p])
        top = jnp.full((ATOMS, LANES), -1e30, F32)
        for j in range(ATOMS):
            at = pl.ds(j * ATOMS, ATOMS)
            score = s.attn[p, at, :]
            for d in range(HEAD_DIM):
                lanes = pl.ds(d * LANES, LANES)
                score = score + s.q[p, :, lanes] * s.k[p, j : j + 1, lanes]
            score = jnp.where(j < count, score, -1e30)
            s.attn[p, at, :] = score
            top = jnp.maximum(top, score)
        total = jnp.zeros((ATOMS, LANES), F32)
        for j in range(ATOMS):
            at = pl.ds(j * ATOMS, ATOMS)
            expo = jnp.exp(s.attn[p, at, :] - top)
            s.attn[p, at, :] = expo
            total = total + expo
        real = lax.broadcasted_iota(jnp.int32, (ATOMS, LANES), 0) < count
        share = jnp.where(real, 1.0 / total, 0.0)
        for j in range(ATOMS):
            at = pl.ds(j * ATOMS, ATOMS)
            weight = s.attn[p, at, :] * share
            s.attn[p, at, :] = weight
            s.column[p, j : j + 1, :] = jnp.sum(weight, axis=0, keepdims=True)
        odd_row = lane_is_odd((1, LANES))
        for d in range(HEAD_DIM):
            lanes = pl.ds(d * LANES, LANES)
            context = jnp.sum(s.column[p] * s.v[p, :, lanes], axis=0, keepdims=True)
            s.context[2 * p, :, lanes] = jnp.where(odd_row, 0.0, context)
            s.context[2 * p + 1, :, lanes] = jnp.where(odd_row, context, 0.0)
        return carry

    lax.fori_loop(0, PAIRS, one_pair, 0)

def pool(wout, proj, s):
    context = jnp.concatenate([s.context[m] for m in range(MOLS)], axis=0)
    context = two_part(context, s.perm[...], mm_t)
    s.ctx_sum[...] = context
    pooled = (s.xsum[...] + two_part(context, wout[...], mm)).astype(BF)
    s.pooled[...] = pooled.astype(F32)
    return mm(pooled, proj[...])


def start_backward(grad_z3, wout, proj, s):
    cs_high, cs_low = halves(s.ctx_sum[...])
    g_high, g_low = halves(grad_z3)
    f = lambda v: v.astype(F32)
    left = jnp.concatenate([f(cs_high), f(cs_low), f(cs_high)], axis=0).astype(BF)
    right = jnp.concatenate([f(g_high), f(g_high), f(g_low)], axis=0).astype(BF)
    s.payload[:, CTX:HEAD] = tmm(left, right).astype(BF)
    left = jnp.concatenate([s.pooled[...], s.pooled[...]], axis=0).astype(BF)
    right = jnp.concatenate([f(g_high), f(g_low)], axis=0).astype(BF)
    s.payload[:, HEAD:QUERY] = tmm(left, right).astype(BF)

    grad_pooled = two_part(grad_z3, proj[...], mm_t)
    grad_ctx = two_part(grad_pooled, wout[...], mm_t)
    spread = two_part(grad_ctx, s.perm[...], mm)
    for m in range(MOLS):
        s.context[m] = spread[m : m + 1]


def value_backward(s):
    odd_row = lane_is_odd((1, LANES))

    def one_pair(p, carry):
        along = jnp.zeros((ATOMS, LANES), F32)
        for d in range(HEAD_DIM):
            lanes = pl.ds(d * LANES, LANES)
            grad = jnp.where(odd_row, s.context[2 * p + 1, :, lanes], s.context[2 * p, :, lanes])
            along = along + grad * s.v[p, :, lanes]
            s.dv[p, :, lanes] = (s.column[p] * grad).astype(BF)
        s.along[p] = along
        return carry

    lax.fori_loop(0, PAIRS, one_pair, 0)


def attend_backward(s):
    scale = HEAD_DIM ** (-0.5)

    def one_pair(p, carry):
        mean = jnp.zeros((ATOMS, LANES), F32)
        for j in range(ATOMS):
            mean = mean + s.attn[p, pl.ds(j * ATOMS, ATOMS), :] * s.along[p, j : j + 1, :]
        for half in range(2):
            ds_range = range(4 * half, 4 * half + 4)
            sums = [jnp.zeros((ATOMS, LANES), F32) for d in ds_range]
            for j in range(ATOMS):
                at = pl.ds(j * ATOMS, ATOMS)
                if half == 0:
                    slope = s.attn[p, at, :] * (s.along[p, j : j + 1, :] - mean)
                    s.attn[p, at, :] = slope
                else:
                    slope = s.attn[p, at, :]
                for n, d in enumerate(ds_range):
                    lanes = pl.ds(d * LANES, LANES)
                    sums[n] = sums[n] + slope * s.k[p, j : j + 1, lanes]
                    s.dk[j : j + 1, lanes] = jnp.sum(slope * s.q[p, :, lanes], axis=0, keepdims=True)
            for n, d in enumerate(ds_range):
                s.dqs[p, :, pl.ds(d * LANES, LANES)] = (sums[n] * scale).astype(BF)
        s.dks[p] = s.dk[...].astype(BF)
        return carry

    lax.fori_loop(0, PAIRS, one_pair, 0)


def bias_backward(s):
    bias_sum = jnp.zeros((2 * KERNELS, LANES), F32)
    for p in range(PAIRS):
        bias_sum = bias_sum + mm(s.basis[p], s.attn[p].astype(BF))
    odd = lane_is_odd((KERNELS, LANES))
    folded = jnp.where(odd, bias_sum[KERNELS:], bias_sum[:KERNELS]).T
    s.small[...] = jnp.zeros((WIDTH, LANES), F32)
    s.small[0:64, :] = folded[:64] + folded[64:]


def project_backward(source, part, target, s):
    odd = lane_is_odd((ATOMS, WIDE))
    zero = jnp.zeros((ATOMS, WIDE), BF)
    pieces = []
    for m in range(MOLS):
        value = source[m // 2]
        pieces.append(jnp.where(odd, value, zero) if m % 2 else jnp.where(odd, zero, value))
    dproj = mm_t(jnp.concatenate(pieces, axis=0), s.perm[...]).astype(BF)
    s.dproj[:, part * WIDTH : (part + 1) * WIDTH] = dproj
    s.payload[:, target : target + WIDTH] = tmm(s.normed[...], dproj).astype(BF)


def gain_backward(wqkv, s):
    grad_normed = mm_t(s.dproj[...], wqkv[...])
    grad_gain = jnp.sum(grad_normed * s.xhat[...], axis=0, keepdims=True)
    for n in range(4):
        s.small[64 + n : 65 + n, :] = grad_gain[:, n * LANES : (n + 1) * LANES]


def fused(
    counts,
    positives,
    feats_in,
    coords,
    z2,
    wqkv_in,
    wout_in,
    proj_in,
    bias_t,
    gain,
    summed_out,
    grad_z2,
    *scratch,
):
    s = Scratch(scratch)
    sems = (s.send, s.recv)
    loads = [
        pltpu.make_async_copy(src, dst, s.load.at[n])
        for n, (src, dst) in enumerate(
            ((feats_in, s.feats), (wqkv_in, s.wqkv), (wout_in, s.wout), (proj_in, s.proj))
        )
    ]
    for load in loads:
        load.start()
    feats, wqkv, wout, proj = s.feats, s.wqkv, s.wout, s.proj

    dp, y_high = lax.axis_index("dp"), lax.axis_index("group")
    bits = [(dp // 2**n) % 2 for n in range(7)]
    cross = [2**n * (1 - 2 * bits[n]) for n in range(7)]
    cross_y = 1 - 2 * y_high
    core = bits[0]
    x_at = bits[1] + 2 * bits[2]
    y_at = bits[3] * 2 + y_high
    ring = dp // 16
    plane = y_high + 2 * x_at + 8 * bits[3]
    depth = core + 2 * ring
    along_row = subsets(
        ((0, cross_y, cross_y), (cross[1], 0, cross[1]), (cross[2], 0, cross[2]), (cross[3], 0, cross[3])),
        (dp, y_high, plane),
    )
    along_col = subsets(
        (
            (cross[0], 0, cross[0]),
            (cross[4], 0, 2 * (1 - 2 * bits[4])),
            (cross[5], 0, 4 * (1 - 2 * bits[5])),
            (cross[6], 0, 8 * (1 - 2 * bits[6])),
        ),
        (dp, y_high, depth),
    )
    along_x = subsets(
        ((cross[1], 0, 1 - 2 * bits[1]), (cross[2], 0, 2 * (1 - 2 * bits[2]))), (dp, y_high, x_at)
    )
    along_y = subsets(
        ((0, cross_y, cross_y), (cross[3], 0, 2 * (1 - 2 * bits[3]))), (dp, y_high, y_at)
    )
    along_ring = along_col[0::2]
    sibling = along_col[1][:2]

    barrier = pltpu.get_barrier_semaphore()
    for place in along_row[1:] + along_col[1:]:
        pl.semaphore_signal(barrier, inc=1, device_id=place[:2], device_id_type=MESH)

    loads[0].wait()
    normalize(feats, counts, gain, s)
    make_perm(s)
    loads[1].wait()
    project(wqkv, s)
    pl.semaphore_wait(barrier, 2 * (SIDE - 1))

    def slot(n):
        return pl.ds(n * 8, 8)

    others = range(1, SIDE)

    def start(copy, offsets=others):
        for o in offsets:
            copy(o).start()

    def all_of(ref, kind):
        return remote(ref, ref, sems, kind, sibling)

    def wait(ref, kind):
        all_of(ref, kind).wait()

    s.z2[slot(depth), :] = z2[...].astype(F32)
    targets = jnp.zeros((8, LANES), jnp.int32)
    sub = lax.broadcasted_iota(jnp.int32, (8, LANES), 0)
    for n in range(8):
        targets = jnp.where(sub == n, positives[n], targets)
    s.pos[slot(plane), :] = targets

    def z2_copy(o):
        mine = s.z2.at[slot(depth), :]
        return remote(mine, mine, sems, Z2, along_col[o][:2])

    def pos_copy(o):
        mine = s.pos.at[slot(plane), :]
        return remote(mine, mine, sems, POS, along_row[o][:2])

    def z3_copy(o):
        mine = s.z3.at[slot(plane), :]
        return remote(mine, mine, sems, Z3, along_row[o][:2])

    def rows_copy(o):
        mine = s.rows.at[plane]
        return remote(mine, mine, sems, ROWS, along_row[o][:2])

    def cols_copy(o):
        mine = s.cols.at[depth]
        return remote(mine, mine, sems, COLS, along_col[o][:2])

    def unit_copy(o):
        peer = along_row[o]
        return remote(s.unit.at[peer[2]], s.unit_in.at[plane], sems, UNIT, peer[:2])

    def gz2_copy(o):
        peer = along_col[o]
        return remote(s.gz2.at[peer[2]], s.gz2_in.at[depth], sems, GZ2, peer[:2])

    start(z2_copy)
    start(pos_copy)

    distances(coords, s)
    bias_matrix(bias_t, s)
    pair_biases(s)
    attend(counts, s)
    loads[2].wait()
    loads[3].wait()
    z3 = pool(wout, proj, s)
    inverse = lax.rsqrt(jnp.mean(z3 * z3, axis=1, keepdims=True) + 1e-06) * LANES ** (-0.5)
    s.z3[slot(plane), :] = (z3 * inverse).astype(BF).astype(F32)
    start(z3_copy)
    wait(s.z2.at[pl.ds(0, 120), :], Z2)
    wait(s.pos.at[pl.ds(0, 120), :], POS)
    wait(s.z3.at[pl.ds(0, 120), :], Z3)

    z3_all = s.z3[...].astype(BF)
    z2_all = s.z2[...].astype(BF)
    logits = mm_t(z3_all, z2_all)
    expo = jnp.exp(logits)
    expo_t = jnp.exp(mm_t(z2_all, z3_all))
    s.rows[plane] = jnp.broadcast_to(jnp.sum(expo_t, axis=0, keepdims=True), (8, LANES))
    s.cols[depth] = jnp.broadcast_to(jnp.sum(expo, axis=0, keepdims=True), (8, LANES))
    start(rows_copy)
    start(cols_copy)
    lane = lax.broadcasted_iota(jnp.int32, (LANES, LANES), 1)
    owner = (lane >> 4) * 32 + ((lane >> 3) & 1) * 2 + (dp * 2 + y_high - ring * 32 - core * 2)
    column_id = owner * 8 + (lane & 7)
    hit = s.pos[...] == column_id
    score = jnp.sum(jnp.where(hit, logits, 0.0), axis=0, keepdims=True)
    wait(s.rows.at[pl.ds(0, 15)], ROWS)
    wait(s.cols.at[pl.ds(0, 15)], COLS)
    row_sum = s.rows[0]
    col_sum = s.cols[0]
    for n in range(1, SIDE):
        row_sum = row_sum + s.rows[n]
        col_sum = col_sum + s.cols[n]
    row_half = jnp.broadcast_to(0.5 / row_sum[0:1], (LANES, LANES)).T
    slope = expo * (row_half + 0.5 / col_sum[0:1]) - jnp.where(hit, 1.0, 0.0)
    unit = mm(slope.astype(BF), z2_all)
    for n in range(SIDE):
        s.unit[n] = unit[n * 8 : (n + 1) * 8]
    s.unit_in[plane] = s.unit[plane]
    start(unit_copy)
    grad_cols = tmm(slope.astype(BF), z3_all)
    for n in range(SIDE):
        s.gz2[n] = grad_cols[n * 8 : (n + 1) * 8]
    s.gz2_in[depth] = s.gz2[depth]
    start(gz2_copy)
    one_lane = lax.broadcasted_iota(jnp.int32, (1, LANES), 1)
    row_term = jnp.where((one_lane >> 3) == plane, 0.5 * jnp.log(row_sum[0:1]), 0.0)
    col_term = jnp.where((one_lane >> 3) == depth, 0.5 * jnp.log(col_sum[0:1]), 0.0)
    loss_terms = row_term + col_term - score

    wait(s.unit_in.at[pl.ds(0, 15)], UNIT)
    grad_unit = s.unit_in[0]
    for n in range(1, SIDE):
        grad_unit = grad_unit + s.unit_in[n]
    dot = jnp.sum(z3 * grad_unit, axis=1, keepdims=True)
    grad_z3 = inverse * (grad_unit - z3 * dot * (inverse * inverse))

    summed = s.summed
    ways = ((along_x, x_at, along_y, y_at), (along_y, y_at, along_x, x_at))

    def lanes_of(c, h):
        return pl.ds(CHUNKS[c][h][0], CHUNKS[c][h][1] - CHUNKS[c][h][0])

    def whole(c):
        return pl.ds(CHUNKS[c][0][0], CHUNKS[c][1][1] - CHUNKS[c][0][0])

    def core_copy(c):
        theirs = s.payload.at[pl.ds((1 - core) * 256, 256), whole(c)]
        return remote(theirs, s.core_in.at[:, whole(c)], sems, CORE + c, sibling)

    def first_copy(c, h, o):
        peer, lanes = ways[h][0][o], lanes_of(c, h)
        return remote(
            s.first_out.at[pl.ds(peer[2] * 64, 64), lanes],
            s.first_in.at[ways[h][1], :, lanes],
            sems,
            FIRST + 2 * c + h,
            peer[:2],
        )

    def second_copy(c, h, o):
        peer, lanes = ways[h][2][o], lanes_of(c, h)
        return remote(
            s.second_out.at[pl.ds(peer[2] * 16, 16), lanes],
            s.second_in.at[ways[h][3], :, lanes],
            sems,
            SECOND + 2 * c + h,
            peer[:2],
        )

    def ring_copy(c, h, o):
        lanes = lanes_of(c, h)
        return remote(
            s.ring_out.at[:, lanes],
            s.ring_in.at[ring, :, lanes],
            sems,
            RING + 2 * c + h,
            along_ring[o][:2],
        )

    def second_share(c, h, o):
        mine = summed.at[pl.ds(core * 256 + ways[h][1] * 64 + ways[h][3] * 16, 16), lanes_of(c, h)]
        return remote(mine, mine, sems, SHARE_SECOND + 2 * c + h, ways[h][2][o][:2])

    def first_share(c, h, o):
        mine = summed.at[pl.ds(core * 256 + ways[h][1] * 64, 64), lanes_of(c, h)]
        return remote(mine, mine, sems, SHARE_FIRST + 2 * c + h, ways[h][0][o][:2])

    def core_share(c, h):
        mine = summed.at[pl.ds(core * 256, 256), lanes_of(c, h)]
        return remote(mine, mine, sems, CORE_OUT + 2 * c + h, sibling)

    def store_copy(c):
        return pltpu.make_async_copy(
            summed.at[:, whole(c)], summed_out.at[:, whole(c)], s.load.at[4 + c]
        )

    near, far = range(1, 4), range(1, DEPTH)

    def all_first(c, h):
        return all_of(s.first_in.at[pl.ds(0, 3), :, lanes_of(c, h)], FIRST + 2 * c + h)

    def all_second(c, h):
        return all_of(s.second_in.at[pl.ds(0, 3), :, lanes_of(c, h)], SECOND + 2 * c + h)

    def all_ring(c, h):
        return all_of(s.ring_in.at[pl.ds(0, 7), :, lanes_of(c, h)], RING + 2 * c + h)

    def all_second_share(c, h):
        return all_of(s.second_in.at[pl.ds(0, 3), :, lanes_of(c, h)], SHARE_SECOND + 2 * c + h)

    def all_first_share(c, h):
        return all_of(s.first_in.at[pl.ds(0, 3), :, lanes_of(c, h)], SHARE_FIRST + 2 * c + h)

    def added(ref, count, lanes):
        total = ref[0, :, lanes].astype(F32)
        for n in range(1, count):
            total = total + ref[n, :, lanes].astype(F32)
        return total.astype(BF)

    def first_step(c):
        core_copy(c).wait_recv()
        mine = s.payload[pl.ds(core * 256, 256), whole(c)].astype(F32)
        s.first_out[:, whole(c)] = (mine + s.core_in[:, whole(c)].astype(F32)).astype(BF)
        for h in range(2):
            for o in near:
                first_copy(c, h, o).start()
        for h in range(2):
            lanes, at = lanes_of(c, h), ways[h][1]
            s.first_in[at, :, lanes] = s.first_out[pl.ds(at * 64, 64), lanes]

    def second_step(c):
        for h in range(2):
            lanes, at = lanes_of(c, h), ways[h][3]
            all_first(c, h).wait_recv()
            s.second_out[:, lanes] = added(s.first_in, 4, lanes)
            for o in near:
                second_copy(c, h, o).start()
            s.second_in[at, :, lanes] = s.second_out[pl.ds(at * 16, 16), lanes]

    def ring_step(c):
        for h in range(2):
            lanes = lanes_of(c, h)
            all_second(c, h).wait_recv()
            total = added(s.second_in, 4, lanes)
            s.ring_out[:, lanes] = total
            for o in far:
                ring_copy(c, h, o).start()
            s.ring_in[ring, :, lanes] = total

    def share_second_step(c):
        for h in range(2):
            lanes = lanes_of(c, h)
            all_ring(c, h).wait_recv()
            at = pl.ds(core * 256 + ways[h][1] * 64 + ways[h][3] * 16, 16)
            summed[at, lanes] = added(s.ring_in, DEPTH, lanes)
            for o in near:
                second_share(c, h, o).start()

    def share_first_step(c):
        for h in range(2):
            all_second_share(c, h).wait_recv()
            for o in near:
                first_share(c, h, o).start()

    def share_core_step(c):
        for h in range(2):
            all_first_share(c, h).wait_recv()
            core_share(c, h).start()

    def store_step(c):
        for h in range(2):
            core_share(c, h).wait_recv()
        store_copy(c).start()

    start_backward(grad_z3, wout, proj, s)
    value_backward(s)
    project_backward(s.dv, 2, VALUE, s)
    core_copy(0).start()
    attend_backward(s)
    first_step(0)
    project_backward(s.dqs, 0, QUERY, s)
    project_backward(s.dks, 1, KEY, s)
    core_copy(1).start()
    bias_backward(s)
    second_step(0)
    first_step(1)
    gain_backward(wqkv, s)
    s.small[68:69, :] = loss_terms
    s.payload[:, SMALL:PAYLOAD] = s.small[...].astype(BF)
    core_copy(2).start()
    ring_step(0)
    first_step(2)
    second_step(1)
    second_step(2)
    ring_step(1)
    share_second_step(0)
    ring_step(2)
    share_first_step(0)
    share_second_step(1)
    share_core_step(0)
    share_first_step(1)
    share_second_step(2)
    store_step(0)
    share_core_step(1)
    share_first_step(2)
    store_step(1)
    share_core_step(2)

    wait(s.gz2_in.at[pl.ds(0, 15)], GZ2)
    total = s.gz2_in[0]
    for n in range(1, SIDE):
        total = total + s.gz2_in[n]
    grad_z2[...] = total
    store_step(2)
    for c in range(3):
        core_copy(c).wait_send()
        for h in range(2):
            for group in (all_first, all_second, all_ring, all_second_share, all_first_share):
                group(c, h).wait_send()
            core_share(c, h).wait_send()
    for c in range(3):
        store_copy(c).wait()


SHAPES = {
    "xhat": ((256, WIDTH), F32),
    "normed": ((256, WIDTH), BF),
    "xsum": ((MOLS, WIDTH), F32),
    "perm": ((WIDTH, WIDE), BF),
    "q": ((PAIRS, ATOMS, WIDE), F32),
    "k": ((PAIRS, ATOMS, WIDE), F32),
    "v": ((PAIRS, ATOMS, WIDE), F32),
    "distance": ((MOLS, 1, ATOMS * ATOMS), F32),
    "bias_lhs": ((2 * LANES, 2 * KERNELS), BF),
    "basis": ((PAIRS, 2 * KERNELS, ATOMS * ATOMS), BF),
    "attn": ((PAIRS, ATOMS * ATOMS, LANES), F32),
    "column": ((PAIRS, ATOMS, LANES), F32),
    "context": ((MOLS, 1, WIDE), F32),
    "ctx_sum": ((MOLS, WIDTH), F32),
    "pooled": ((MOLS, WIDTH), F32),
    "along": ((PAIRS, ATOMS, LANES), F32),
    "dk": ((ATOMS, WIDE), F32),
    "dqs": ((PAIRS, ATOMS, WIDE), BF),
    "dks": ((PAIRS, ATOMS, WIDE), BF),
    "dv": ((PAIRS, ATOMS, WIDE), BF),
    "dproj": ((256, 3 * WIDTH), BF),
    "small": ((WIDTH, LANES), F32),
    "payload": ((WIDTH, PAYLOAD), BF),
    "z2": ((LANES, LANES), F32),
    "pos": ((LANES, LANES), jnp.int32),
    "z3": ((LANES, LANES), F32),
    "rows": ((SIDE, 8, LANES), F32),
    "cols": ((SIDE, 8, LANES), F32),
    "unit": ((SIDE, 8, LANES), F32),
    "unit_in": ((SIDE, 8, LANES), F32),
    "gz2": ((SIDE, 8, LANES), F32),
    "gz2_in": ((SIDE, 8, LANES), F32),
    "core_in": ((256, PAYLOAD), BF),
    "first_out": ((256, PAYLOAD), BF),
    "first_in": ((4, 64, PAYLOAD), BF),
    "second_out": ((64, PAYLOAD), BF),
    "second_in": ((4, 16, PAYLOAD), BF),
    "ring_out": ((16, PAYLOAD), BF),
    "ring_in": ((DEPTH, 16, PAYLOAD), BF),
    "summed": ((WIDTH, PAYLOAD), BF),
    "feats": ((256, WIDTH), BF),
    "wqkv": ((WIDTH, 3 * WIDTH), BF),
    "wout": ((WIDTH, WIDTH), BF),
    "proj": ((WIDTH, LANES), BF),
}


class Scratch:
    def __init__(self, refs):
        for name, ref in zip(list(SHAPES) + ["send", "recv", "load"], refs):
            setattr(self, name, ref)


def unpack(summed, proj, cols_in, loss, cols_out, g_qkv, g_out, g_proj, g_bias, g_gain):
    for part, start in enumerate((QUERY, KEY, VALUE)):
        g_qkv[:, part * WIDTH : (part + 1) * WIDTH] = summed[:, start : start + WIDTH].astype(F32)
    g_out[...] = mm_t(summed[:, CTX:HEAD], proj[...])
    g_proj[...] = summed[:, HEAD:QUERY].astype(F32)
    cols_out[...] = cols_in[...]
    g_bias[...] = summed[0:64, SMALL:PAYLOAD].astype(F32)
    small = summed[64:80, SMALL:PAYLOAD].astype(F32)
    for n in range(4):
        g_gain[:, n * LANES : (n + 1) * LANES] = small[n : n + 1]
    loss[...] = jnp.sum(small[4:5], axis=1, keepdims=True) / BATCH


def on_device(
    atom_feats, coords, atom_counts, positives, z2, w_qkv, w_out, proj, bias_weight, ln_gain
):
    vmem = pl.BlockSpec(memory_space=pltpu.VMEM)
    smem = pl.BlockSpec(memory_space=pltpu.SMEM)
    hbm = pl.BlockSpec(memory_space=pl.ANY)
    summed, grad_z2 = pl.pallas_call(
        fused,
        out_shape=(
            jax.ShapeDtypeStruct((WIDTH, PAYLOAD), BF),
            jax.ShapeDtypeStruct((8, LANES), F32),
        ),
        in_specs=[smem, smem, hbm, vmem, vmem, hbm, hbm, hbm, vmem, vmem],
        out_specs=(hbm, vmem),
        scratch_shapes=[pltpu.VMEM(*shape) for shape in SHAPES.values()]
        + [pltpu.SemaphoreType.DMA((KINDS,))] * 2
        + [pltpu.SemaphoreType.DMA((7,))],
        compiler_params=pltpu.CompilerParams(
            collective_id=0, has_side_effects=True, vmem_limit_bytes=56 * 1024 * 1024
        ),
        name="pretrain_step",
    )(
        atom_counts,
        positives,
        atom_feats.reshape(256, WIDTH),
        coords.transpose(1, 0, 2),
        z2,
        w_qkv,
        w_out,
        proj,
        bias_weight.T,
        ln_gain.reshape(1, WIDTH),
    )
    shapes = ((1, 1), (8, LANES), (WIDTH, 3 * WIDTH), (WIDTH, WIDTH), (WIDTH, LANES), (HEADS, KERNELS), (1, WIDTH))
    loss, grad_z2, g_qkv, g_out, g_proj, g_bias, g_gain = pl.pallas_call(
        unpack,
        out_shape=tuple(jax.ShapeDtypeStruct(shape, F32) for shape in shapes),
        in_specs=[vmem] * 3,
        out_specs=(vmem,) * 7,
        compiler_params=pltpu.CompilerParams(vmem_limit_bytes=56 * 1024 * 1024),
        name="unpack",
    )(summed, proj, grad_z2)
    return (loss.reshape(()), grad_z2, g_qkv, g_out, g_proj, g_bias.T, g_gain.reshape(WIDTH))


def solution(mesh):
    return jax.shard_map(
        on_device,
        mesh=mesh,
        in_specs=(
            P(("dp", "group"), None, None),
            P(("dp", "group"), None, None),
            P(("dp", "group")),
            P(("dp", "group")),
            P(("dp", "group"), None),
            P(),
            P(),
            P(),
            P(),
            P(),
        ),
        out_specs=(P(), P(("dp", "group"), None), P(), P(), P(), P(), P()),
        check_vma=False,
    )
```

```python
import functools

import jax
import jax.numpy as jnp
from jax import lax
from jax.experimental import pallas as pl
from jax.experimental.pallas import tpu as pltpu
from jax.sharding import PartitionSpec as P

MESH = pl.DeviceIdType.MESH
F32 = jnp.float32
BF = jnp.bfloat16

MOLS = 8
PAIRS = 4
ATOMS = 32
WIDTH = 512
HEADS = 64
HEAD_DIM = 8
KERNELS = 128
LANES = 128
WIDE = HEAD_DIM * LANES
BATCH = 2048
SIDE = 16
DEPTH = 8

VALUE, CTX, HEAD, QUERY, KEY, SMALL, PAYLOAD = 0, 512, 640, 768, 1280, 1792, 1920
CHUNKS = (((0, 384), (384, 768)), ((768, 1152), (1152, 1536)), ((1536, 1792), (1792, 1920)))

Z2, POS, Z3, ROWS, COLS, UNIT, GZ2 = range(7)
FIRST, SECOND, RING, SHARE_SECOND, SHARE_FIRST, CORE_OUT = (7 + 6 * n for n in range(6))
CORE = 43
KINDS = CORE + 3


def mm(a, b):
    return lax.dot_general(a, b, (((1,), (0,)), ((), ())), preferred_element_type=F32)


def mm_t(a, b):
    return lax.dot_general(a, b, (((1,), (1,)), ((), ())), preferred_element_type=F32)


def tmm(a, b):
    return lax.dot_general(a, b, (((0,), (0,)), ((), ())), preferred_element_type=F32)


def halves(values):
    high = values.astype(BF)
    return high, (values - high.astype(F32)).astype(BF)


def stacked(values):
    high = values.astype(BF).astype(F32)
    return jnp.concatenate([high, values - high], axis=0).astype(BF)


def two_part(values, weights, product):
    rows = values.shape[0]
    both = product(stacked(values), weights)
    return both[:rows] + both[rows:]


def lane_is_odd(shape):
    return (lax.broadcasted_iota(jnp.int32, shape, len(shape) - 1) & 64) != 0


def remote(src, dst, sems, kind, device):
    return pltpu.make_async_remote_copy(
        src_ref=src,
        dst_ref=dst,
        send_sem=sems[0].at[kind],
        recv_sem=sems[1].at[kind],
        device_id=device,
        device_id_type=MESH,
    )


def subsets(flips, start):
    places = [start]
    for flip in flips:
        places = places + [tuple(p + f for p, f in zip(place, flip)) for place in places]
    return places


def normalize(feats, counts, gain, s):
    x = feats[...].astype(F32)
    mean = jnp.mean(x, axis=-1, keepdims=True)
    centred = x - mean
    var = jnp.mean(centred * centred, axis=-1, keepdims=True)
    xhat = centred * lax.rsqrt(var + 1e-05)
    s.xhat[...] = xhat
    normed = (xhat * gain[...]).astype(BF)
    s.normed[...] = normed
    for m in range(MOLS):
        valid = lax.broadcasted_iota(jnp.int32, (ATOMS, WIDTH), 0) < counts[m]
        s.xsum[m : m + 1, :] = jnp.sum(
            jnp.where(valid, x[m * ATOMS : (m + 1) * ATOMS], 0.0), axis=0, keepdims=True
        )


def make_perm(s):
    row = lax.broadcasted_iota(jnp.int32, (WIDTH, WIDE), 0)
    col = lax.broadcasted_iota(jnp.int32, (WIDTH, WIDE), 1)
    placed = ((row >> 3) == (col & 63)) & ((row & 7) == (col >> 7))
    s.perm[...] = jnp.where(placed, 1.0, 0.0).astype(BF)


def project(wqkv, s):
    normed = s.normed[...]
    odd = lane_is_odd((ATOMS, WIDE))
    for part, (target, scale) in enumerate(((s.q, HEAD_DIM ** (-0.5)), (s.k, 1.0), (s.v, 1.0))):
        projected = mm(normed, wqkv[:, part * WIDTH : (part + 1) * WIDTH]).astype(BF)
        spread = mm(projected, s.perm[...])
        for p in range(PAIRS):
            low = spread[(2 * p) * ATOMS : (2 * p + 1) * ATOMS]
            high = spread[(2 * p + 1) * ATOMS : (2 * p + 2) * ATOMS]
            merged = jnp.where(odd, high, low)
            target[p] = merged * scale if scale != 1.0 else merged


def distances(coords, s):
    atom = lax.broadcasted_iota(jnp.int32, (ATOMS, ATOMS * ATOMS), 0)
    pair = lax.broadcasted_iota(jnp.int32, (ATOMS, ATOMS * ATOMS), 1)
    select = (
        jnp.where(atom == (pair & 31), 1.0, 0.0) - jnp.where(atom == (pair >> 5), 1.0, 0.0)
    ).astype(BF)
    squared = jnp.zeros((MOLS, ATOMS * ATOMS), F32)
    for c in range(3):
        values = coords[c]
        first = values.astype(BF).astype(F32)
        second = (values - first).astype(BF).astype(F32)
        third = values - first - second
        three = mm(jnp.concatenate([first, second, third], axis=0).astype(BF), select)
        offset = three[:MOLS] + three[MOLS : 2 * MOLS] + three[2 * MOLS :]
        squared = squared + offset * offset
    distance = jnp.sqrt(squared + 0.25)
    for m in range(MOLS):
        s.distance[m] = distance[m : m + 1]


def bias_matrix(bias_t, s):
    turned = jnp.concatenate([bias_t[...], bias_t[...]], axis=0)
    upper = lax.broadcasted_iota(jnp.int32, (LANES, KERNELS), 0) < HEADS
    blocks = jnp.concatenate([jnp.where(upper, turned, 0.0), jnp.where(upper, 0.0, turned)], axis=1)
    s.bias_lhs[...] = stacked(blocks)


def pair_biases(s):
    centers = lax.broadcasted_iota(jnp.int32, (KERNELS, 2 * LANES), 0).astype(F32) * (12.0 / KERNELS)

    def one_pair(p, carry):
        for block in range(4):
            at = pl.ds(block * 256, 256)
            basis = []
            for parity in range(2):
                away = (s.distance[2 * p + parity, :, at] - centers) * 2.0
                basis.append(jnp.exp(-(away * away)))
            high, low = halves(jnp.concatenate(basis, axis=0))
            s.basis[p, :, at] = high
            both = mm(s.bias_lhs[...], high)
            bias = both[:LANES] + both[LANES:] + mm(s.bias_lhs[:LANES, :], low)
            s.attn[p, at, :] = bias.T
        return carry

    lax.fori_loop(0, PAIRS, one_pair, 0, unroll=True)


def attend(counts, s):
    def one_pair(p, carry):
        count = jnp.where(lane_is_odd((1, LANES)), counts[2 * p + 1], counts[2 * p])
        top = jnp.full((ATOMS, LANES), -1e30, F32)
        for j in range(ATOMS):
            at = pl.ds(j * ATOMS, ATOMS)
            score = s.attn[p, at, :]
            for d in range(HEAD_DIM):
                lanes = pl.ds(d * LANES, LANES)
                score = score + s.q[p, :, lanes] * s.k[p, j : j + 1, lanes]
            score = jnp.where(j < count, score, -1e30)
            s.attn[p, at, :] = score
            top = jnp.maximum(top, score)
        total = jnp.zeros((ATOMS, LANES), F32)
        for j in range(ATOMS):
            at = pl.ds(j * ATOMS, ATOMS)
            expo = jnp.exp(s.attn[p, at, :] - top)
            s.attn[p, at, :] = expo
            total = total + expo
        real = lax.broadcasted_iota(jnp.int32, (ATOMS, LANES), 0) < count
        share = jnp.where(real, 1.0 / total, 0.0)
        for j in range(ATOMS):
            at = pl.ds(j * ATOMS, ATOMS)
            weight = s.attn[p, at, :] * share
            s.attn[p, at, :] = weight
            s.column[p, j : j + 1, :] = jnp.sum(weight, axis=0, keepdims=True)
        odd_row = lane_is_odd((1, LANES))
        for d in range(HEAD_DIM):
            lanes = pl.ds(d * LANES, LANES)
            context = jnp.sum(s.column[p] * s.v[p, :, lanes], axis=0, keepdims=True)
            s.context[2 * p, :, lanes] = jnp.where(odd_row, 0.0, context)
            s.context[2 * p + 1, :, lanes] = jnp.where(odd_row, context, 0.0)
        return carry

    lax.fori_loop(0, PAIRS, one_pair, 0, unroll=True)

def pool(wout, proj, s):
    context = jnp.concatenate([s.context[m] for m in range(MOLS)], axis=0)
    context = two_part(context, s.perm[...], mm_t)
    s.ctx_sum[...] = context
    pooled = (s.xsum[...] + two_part(context, wout[...], mm)).astype(BF)
    s.pooled[...] = pooled.astype(F32)
    return mm(pooled, proj[...])


def start_backward(grad_z3, wout, proj, s):
    cs_high, cs_low = halves(s.ctx_sum[...])
    g_high, g_low = halves(grad_z3)
    f = lambda v: v.astype(F32)
    left = jnp.concatenate([f(cs_high), f(cs_low), f(cs_high)], axis=0).astype(BF)
    right = jnp.concatenate([f(g_high), f(g_high), f(g_low)], axis=0).astype(BF)
    s.payload[:, CTX:HEAD] = tmm(left, right).astype(BF)
    left = jnp.concatenate([s.pooled[...], s.pooled[...]], axis=0).astype(BF)
    right = jnp.concatenate([f(g_high), f(g_low)], axis=0).astype(BF)
    s.payload[:, HEAD:QUERY] = tmm(left, right).astype(BF)

    grad_pooled = two_part(grad_z3, proj[...], mm_t)
    grad_ctx = two_part(grad_pooled, wout[...], mm_t)
    spread = two_part(grad_ctx, s.perm[...], mm)
    for m in range(MOLS):
        s.context[m] = spread[m : m + 1]


def value_backward(s):
    odd_row = lane_is_odd((1, LANES))

    def one_pair(p, carry):
        along = jnp.zeros((ATOMS, LANES), F32)
        for d in range(HEAD_DIM):
            lanes = pl.ds(d * LANES, LANES)
            grad = jnp.where(odd_row, s.context[2 * p + 1, :, lanes], s.context[2 * p, :, lanes])
            along = along + grad * s.v[p, :, lanes]
            s.dv[p, :, lanes] = (s.column[p] * grad).astype(BF)
        s.along[p] = along
        return carry

    lax.fori_loop(0, PAIRS, one_pair, 0, unroll=True)


def attend_backward(first, last, s):
    scale = HEAD_DIM ** (-0.5)

    def one_pair(p, carry):
        mean = jnp.zeros((ATOMS, LANES), F32)
        for j in range(ATOMS):
            mean = mean + s.attn[p, pl.ds(j * ATOMS, ATOMS), :] * s.along[p, j : j + 1, :]
        for half in range(2):
            ds_range = range(4 * half, 4 * half + 4)
            sums = [jnp.zeros((ATOMS, LANES), F32) for d in ds_range]
            for j in range(ATOMS):
                at = pl.ds(j * ATOMS, ATOMS)
                if half == 0:
                    slope = s.attn[p, at, :] * (s.along[p, j : j + 1, :] - mean)
                    s.attn[p, at, :] = slope
                else:
                    slope = s.attn[p, at, :]
                for n, d in enumerate(ds_range):
                    lanes = pl.ds(d * LANES, LANES)
                    sums[n] = sums[n] + slope * s.k[p, j : j + 1, lanes]
                    s.dk[j : j + 1, lanes] = jnp.sum(slope * s.q[p, :, lanes], axis=0, keepdims=True)
            for n, d in enumerate(ds_range):
                s.dqs[p, :, pl.ds(d * LANES, LANES)] = (sums[n] * scale).astype(BF)
        s.dks[p] = s.dk[...].astype(BF)
        return carry

    lax.fori_loop(first, last, one_pair, 0, unroll=True)


def bias_backward(s):
    bias_sum = jnp.zeros((2 * KERNELS, LANES), F32)
    for p in range(PAIRS):
        bias_sum = bias_sum + mm(s.basis[p], s.attn[p].astype(BF))
    odd = lane_is_odd((KERNELS, LANES))
    folded = jnp.where(odd, bias_sum[KERNELS:], bias_sum[:KERNELS]).T
    s.small[...] = jnp.zeros((WIDTH, LANES), F32)
    s.small[0:64, :] = folded[:64] + folded[64:]


def project_backward(source, part, target, s):
    odd = lane_is_odd((ATOMS, WIDE))
    zero = jnp.zeros((ATOMS, WIDE), BF)
    pieces = []
    for m in range(MOLS):
        value = source[m // 2]
        pieces.append(jnp.where(odd, value, zero) if m % 2 else jnp.where(odd, zero, value))
    dproj = mm_t(jnp.concatenate(pieces, axis=0), s.perm[...]).astype(BF)
    s.dproj[:, part * WIDTH : (part + 1) * WIDTH] = dproj
    s.payload[:, target : target + WIDTH] = tmm(s.normed[...], dproj).astype(BF)


def gain_backward(wqkv, s):
    grad_normed = mm_t(s.dproj[...], wqkv[...])
    grad_gain = jnp.sum(grad_normed * s.xhat[...], axis=0, keepdims=True)
    for n in range(4):
        s.small[64 + n : 65 + n, :] = grad_gain[:, n * LANES : (n + 1) * LANES]


def fused(
    counts,
    positives,
    feats_in,
    coords,
    z2,
    wqkv_in,
    wout_in,
    proj_in,
    bias_t,
    gain,
    summed,
    grad_z2,
    proj,
    *scratch,
):
    s = Scratch(scratch)
    sems = (s.send, s.recv)
    loads = [
        pltpu.make_async_copy(src, dst, s.load.at[n])
        for n, (src, dst) in enumerate(
            ((feats_in, s.feats), (wqkv_in, s.wqkv), (wout_in, s.wout), (proj_in, proj))
        )
    ]
    for load in loads:
        load.start()
    feats, wqkv, wout = s.feats, s.wqkv, s.wout

    dp, y_high = lax.axis_index("dp"), lax.axis_index("group")
    bits = [(dp // 2**n) % 2 for n in range(7)]
    cross = [2**n * (1 - 2 * bits[n]) for n in range(7)]
    cross_y = 1 - 2 * y_high
    core = bits[0]
    x_at = bits[1] + 2 * bits[2]
    y_at = bits[3] * 2 + y_high
    ring = dp // 16
    plane = y_high + 2 * x_at + 8 * bits[3]
    depth = core + 2 * ring
    along_row = subsets(
        ((0, cross_y, cross_y), (cross[1], 0, cross[1]), (cross[2], 0, cross[2]), (cross[3], 0, cross[3])),
        (dp, y_high, plane),
    )
    along_col = subsets(
        (
            (cross[0], 0, cross[0]),
            (cross[4], 0, 2 * (1 - 2 * bits[4])),
            (cross[5], 0, 4 * (1 - 2 * bits[5])),
            (cross[6], 0, 8 * (1 - 2 * bits[6])),
        ),
        (dp, y_high, depth),
    )
    along_x = subsets(
        ((cross[1], 0, 1 - 2 * bits[1]), (cross[2], 0, 2 * (1 - 2 * bits[2]))), (dp, y_high, x_at)
    )
    along_y = subsets(
        ((0, cross_y, cross_y), (cross[3], 0, 2 * (1 - 2 * bits[3]))), (dp, y_high, y_at)
    )
    along_ring = along_col[0::2]
    sibling = along_col[1][:2]

    barrier = pltpu.get_barrier_semaphore()
    for place in along_row[1:] + along_col[1:]:
        pl.semaphore_signal(barrier, inc=1, device_id=place[:2], device_id_type=MESH)

    loads[0].wait()
    normalize(feats, counts, gain, s)
    make_perm(s)
    loads[1].wait()
    project(wqkv, s)
    distances(coords, s)
    bias_matrix(bias_t, s)
    pair_biases(s)
    pl.semaphore_wait(barrier, 2 * (SIDE - 1))

    def slot(n):
        return pl.ds(n * 8, 8)

    others = range(1, SIDE)

    def start(copy, offsets=others):
        for o in offsets:
            copy(o).start()

    def all_of(ref, kind):
        return remote(ref, ref, sems, kind, sibling)

    def wait(ref, kind):
        all_of(ref, kind).wait()

    s.z2[slot(depth), :] = z2[...].astype(F32)
    targets = jnp.zeros((8, LANES), jnp.int32)
    sub = lax.broadcasted_iota(jnp.int32, (8, LANES), 0)
    for n in range(8):
        targets = jnp.where(sub == n, positives[n], targets)
    s.pos[slot(plane), :] = targets

    def z2_copy(o):
        mine = s.z2.at[slot(depth), :]
        return remote(mine, mine, sems, Z2, along_col[o][:2])

    def pos_copy(o):
        mine = s.pos.at[slot(plane), :]
        return remote(mine, mine, sems, POS, along_row[o][:2])

    def z3_copy(o):
        mine = s.z3.at[slot(plane), :]
        return remote(mine, mine, sems, Z3, along_row[o][:2])

    def rows_copy(o):
        mine = s.rows.at[plane]
        return remote(mine, mine, sems, ROWS, along_row[o][:2])

    def cols_copy(o):
        mine = s.cols.at[depth]
        return remote(mine, mine, sems, COLS, along_col[o][:2])

    def unit_copy(o):
        peer = along_row[o]
        return remote(s.unit.at[peer[2]], s.unit_in.at[plane], sems, UNIT, peer[:2])

    def gz2_copy(o):
        peer = along_col[o]
        return remote(s.gz2.at[peer[2]], s.gz2_in.at[depth], sems, GZ2, peer[:2])

    start(z2_copy)
    start(pos_copy)

    attend(counts, s)
    loads[2].wait()
    loads[3].wait()
    z3 = pool(wout, proj, s)
    inverse = lax.rsqrt(jnp.mean(z3 * z3, axis=1, keepdims=True) + 1e-06) * LANES ** (-0.5)
    s.z3[slot(plane), :] = (z3 * inverse).astype(BF).astype(F32)
    start(z3_copy)
    wait(s.z2.at[pl.ds(0, 120), :], Z2)
    wait(s.pos.at[pl.ds(0, 120), :], POS)
    wait(s.z3.at[pl.ds(0, 120), :], Z3)

    z3_all = s.z3[...].astype(BF)
    z2_all = s.z2[...].astype(BF)
    logits = mm_t(z3_all, z2_all)
    expo = jnp.exp(logits)
    expo_t = jnp.exp(mm_t(z2_all, z3_all))
    s.rows[plane] = jnp.broadcast_to(jnp.sum(expo_t, axis=0, keepdims=True), (8, LANES))
    s.cols[depth] = jnp.broadcast_to(jnp.sum(expo, axis=0, keepdims=True), (8, LANES))
    start(rows_copy)
    start(cols_copy)
    lane = lax.broadcasted_iota(jnp.int32, (LANES, LANES), 1)
    owner = (lane >> 4) * 32 + ((lane >> 3) & 1) * 2 + (dp * 2 + y_high - ring * 32 - core * 2)
    column_id = owner * 8 + (lane & 7)
    hit = s.pos[...] == column_id
    score = jnp.sum(jnp.where(hit, logits, 0.0), axis=0, keepdims=True)
    wait(s.rows.at[pl.ds(0, 15)], ROWS)
    wait(s.cols.at[pl.ds(0, 15)], COLS)
    row_sum = s.rows[0]
    col_sum = s.cols[0]
    for n in range(1, SIDE):
        row_sum = row_sum + s.rows[n]
        col_sum = col_sum + s.cols[n]
    row_half = jnp.broadcast_to(0.5 / row_sum[0:1], (LANES, LANES)).T
    slope = expo * (row_half + 0.5 / col_sum[0:1]) - jnp.where(hit, 1.0, 0.0)
    unit = mm(slope.astype(BF), z2_all)
    for n in range(SIDE):
        s.unit[n] = unit[n * 8 : (n + 1) * 8]
    s.unit_in[plane] = s.unit[plane]
    start(unit_copy)
    grad_cols = tmm(slope.astype(BF), z3_all)
    for n in range(SIDE):
        s.gz2[n] = grad_cols[n * 8 : (n + 1) * 8]
    s.gz2_in[depth] = s.gz2[depth]
    start(gz2_copy)
    one_lane = lax.broadcasted_iota(jnp.int32, (1, LANES), 1)
    row_term = jnp.where((one_lane >> 3) == plane, 0.5 * jnp.log(row_sum[0:1]), 0.0)
    col_term = jnp.where((one_lane >> 3) == depth, 0.5 * jnp.log(col_sum[0:1]), 0.0)
    loss_terms = row_term + col_term - score

    wait(s.unit_in.at[pl.ds(0, 15)], UNIT)
    grad_unit = s.unit_in[0]
    for n in range(1, SIDE):
        grad_unit = grad_unit + s.unit_in[n]
    dot = jnp.sum(z3 * grad_unit, axis=1, keepdims=True)
    grad_z3 = inverse * (grad_unit - z3 * dot * (inverse * inverse))

    ways = ((along_x, x_at, along_y, y_at), (along_y, y_at, along_x, x_at))

    def lanes_of(c, h):
        return pl.ds(CHUNKS[c][h][0], CHUNKS[c][h][1] - CHUNKS[c][h][0])

    def whole(c):
        return pl.ds(CHUNKS[c][0][0], CHUNKS[c][1][1] - CHUNKS[c][0][0])

    def core_copy(c):
        theirs = s.payload.at[pl.ds((1 - core) * 256, 256), whole(c)]
        return remote(theirs, s.core_in.at[:, whole(c)], sems, CORE + c, sibling)

    def first_copy(c, h, o):
        peer, lanes = ways[h][0][o], lanes_of(c, h)
        return remote(
            s.first_out.at[pl.ds(peer[2] * 64, 64), lanes],
            s.first_in.at[ways[h][1], :, lanes],
            sems,
            FIRST + 2 * c + h,
            peer[:2],
        )

    def second_copy(c, h, o):
        peer, lanes = ways[h][2][o], lanes_of(c, h)
        return remote(
            s.second_out.at[pl.ds(peer[2] * 16, 16), lanes],
            s.second_in.at[ways[h][3], :, lanes],
            sems,
            SECOND + 2 * c + h,
            peer[:2],
        )

    def ring_copy(c, h, o):
        lanes = lanes_of(c, h)
        return remote(
            s.ring_out.at[:, lanes],
            s.ring_in.at[ring, :, lanes],
            sems,
            RING + 2 * c + h,
            along_ring[o][:2],
        )

    def second_share(c, h, o):
        mine = summed.at[pl.ds(core * 256 + ways[h][1] * 64 + ways[h][3] * 16, 16), lanes_of(c, h)]
        return remote(mine, mine, sems, SHARE_SECOND + 2 * c + h, ways[h][2][o][:2])

    def first_share(c, h, o):
        mine = summed.at[pl.ds(core * 256 + ways[h][1] * 64, 64), lanes_of(c, h)]
        return remote(mine, mine, sems, SHARE_FIRST + 2 * c + h, ways[h][0][o][:2])

    def core_share(c, h):
        mine = summed.at[pl.ds(core * 256, 256), lanes_of(c, h)]
        return remote(mine, mine, sems, CORE_OUT + 2 * c + h, sibling)

    near, far = range(1, 4), range(1, DEPTH)

    def all_first(c, h):
        return all_of(s.first_in.at[pl.ds(0, 3), :, lanes_of(c, h)], FIRST + 2 * c + h)

    def all_second(c, h):
        return all_of(s.second_in.at[pl.ds(0, 3), :, lanes_of(c, h)], SECOND + 2 * c + h)

    def all_ring(c, h):
        return all_of(s.ring_in.at[pl.ds(0, 7), :, lanes_of(c, h)], RING + 2 * c + h)

    def all_second_share(c, h):
        return all_of(s.second_in.at[pl.ds(0, 3), :, lanes_of(c, h)], SHARE_SECOND + 2 * c + h)

    def all_first_share(c, h):
        return all_of(s.first_in.at[pl.ds(0, 3), :, lanes_of(c, h)], SHARE_FIRST + 2 * c + h)

    def added(ref, count, lanes):
        total = ref[0, :, lanes].astype(F32)
        for n in range(1, count):
            total = total + ref[n, :, lanes].astype(F32)
        return total.astype(BF)

    def first_step(c):
        core_copy(c).wait_recv()
        mine = s.payload[pl.ds(core * 256, 256), whole(c)].astype(F32)
        s.first_out[:, whole(c)] = (mine + s.core_in[:, whole(c)].astype(F32)).astype(BF)
        for h in range(2):
            for o in near:
                first_copy(c, h, o).start()
        for h in range(2):
            lanes, at = lanes_of(c, h), ways[h][1]
            s.first_in[at, :, lanes] = s.first_out[pl.ds(at * 64, 64), lanes]

    def second_step(c):
        for h in range(2):
            lanes, at = lanes_of(c, h), ways[h][3]
            all_first(c, h).wait_recv()
            s.second_out[:, lanes] = added(s.first_in, 4, lanes)
            for o in near:
                second_copy(c, h, o).start()
            s.second_in[at, :, lanes] = s.second_out[pl.ds(at * 16, 16), lanes]

    def ring_step(c):
        for h in range(2):
            lanes = lanes_of(c, h)
            all_second(c, h).wait_recv()
            total = added(s.second_in, 4, lanes)
            s.ring_out[:, lanes] = total
            for o in far:
                ring_copy(c, h, o).start()
            s.ring_in[ring, :, lanes] = total

    def share_second_step(c):
        for h in range(2):
            lanes = lanes_of(c, h)
            all_ring(c, h).wait_recv()
            at = pl.ds(core * 256 + ways[h][1] * 64 + ways[h][3] * 16, 16)
            summed[at, lanes] = added(s.ring_in, DEPTH, lanes)
            for o in near:
                second_share(c, h, o).start()

    def share_first_step(c):
        for h in range(2):
            all_second_share(c, h).wait_recv()
            for o in near:
                first_share(c, h, o).start()

    def share_core_step(c):
        for h in range(2):
            all_first_share(c, h).wait_recv()
            core_share(c, h).start()

    def arrive_step(c):
        for h in range(2):
            core_share(c, h).wait_recv()

    start_backward(grad_z3, wout, proj, s)
    value_backward(s)
    project_backward(s.dv, 2, VALUE, s)
    core_copy(0).start()
    attend_backward(0, 2, s)
    first_step(0)
    attend_backward(2, PAIRS, s)
    project_backward(s.dqs, 0, QUERY, s)
    project_backward(s.dks, 1, KEY, s)
    core_copy(1).start()
    bias_backward(s)
    first_step(1)
    gain_backward(wqkv, s)
    s.small[68:69, :] = loss_terms
    s.payload[:, SMALL:PAYLOAD] = s.small[...].astype(BF)
    core_copy(2).start()
    second_step(0)
    first_step(2)
    ring_step(0)
    second_step(1)
    second_step(2)
    ring_step(1)
    ring_step(2)
    share_second_step(0)
    share_first_step(0)
    share_second_step(1)
    share_second_step(2)
    share_first_step(1)
    share_core_step(0)
    share_first_step(2)
    share_core_step(1)
    arrive_step(0)
    share_core_step(2)
    arrive_step(1)

    wait(s.gz2_in.at[pl.ds(0, 15)], GZ2)
    total = s.gz2_in[0]
    for n in range(1, SIDE):
        total = total + s.gz2_in[n]
    grad_z2[...] = total
    arrive_step(2)
    for c in range(3):
        core_copy(c).wait_send()
        for h in range(2):
            for group in (all_first, all_second, all_ring, all_second_share, all_first_share):
                group(c, h).wait_send()
            core_share(c, h).wait_send()


SHAPES = {
    "xhat": ((256, WIDTH), F32),
    "normed": ((256, WIDTH), BF),
    "xsum": ((MOLS, WIDTH), F32),
    "perm": ((WIDTH, WIDE), BF),
    "q": ((PAIRS, ATOMS, WIDE), F32),
    "k": ((PAIRS, ATOMS, WIDE), F32),
    "v": ((PAIRS, ATOMS, WIDE), F32),
    "distance": ((MOLS, 1, ATOMS * ATOMS), F32),
    "bias_lhs": ((2 * LANES, 2 * KERNELS), BF),
    "basis": ((PAIRS, 2 * KERNELS, ATOMS * ATOMS), BF),
    "attn": ((PAIRS, ATOMS * ATOMS, LANES), F32),
    "column": ((PAIRS, ATOMS, LANES), F32),
    "context": ((MOLS, 1, WIDE), F32),
    "ctx_sum": ((MOLS, WIDTH), F32),
    "pooled": ((MOLS, WIDTH), F32),
    "along": ((PAIRS, ATOMS, LANES), F32),
    "dk": ((ATOMS, WIDE), F32),
    "dqs": ((PAIRS, ATOMS, WIDE), BF),
    "dks": ((PAIRS, ATOMS, WIDE), BF),
    "dv": ((PAIRS, ATOMS, WIDE), BF),
    "dproj": ((256, 3 * WIDTH), BF),
    "small": ((WIDTH, LANES), F32),
    "payload": ((WIDTH, PAYLOAD), BF),
    "z2": ((LANES, LANES), F32),
    "pos": ((LANES, LANES), jnp.int32),
    "z3": ((LANES, LANES), F32),
    "rows": ((SIDE, 8, LANES), F32),
    "cols": ((SIDE, 8, LANES), F32),
    "unit": ((SIDE, 8, LANES), F32),
    "unit_in": ((SIDE, 8, LANES), F32),
    "gz2": ((SIDE, 8, LANES), F32),
    "gz2_in": ((SIDE, 8, LANES), F32),
    "core_in": ((256, PAYLOAD), BF),
    "first_out": ((256, PAYLOAD), BF),
    "first_in": ((4, 64, PAYLOAD), BF),
    "second_out": ((64, PAYLOAD), BF),
    "second_in": ((4, 16, PAYLOAD), BF),
    "ring_out": ((16, PAYLOAD), BF),
    "ring_in": ((DEPTH, 16, PAYLOAD), BF),
    "feats": ((256, WIDTH), BF),
    "wqkv": ((WIDTH, 3 * WIDTH), BF),
    "wout": ((WIDTH, WIDTH), BF),
}


class Scratch:
    def __init__(self, refs):
        for name, ref in zip(list(SHAPES) + ["send", "recv", "load"], refs):
            setattr(self, name, ref)


def unpack(
    summed, cols_in, proj, loss, cols_out, g_qkv, g_out, g_proj, g_bias, g_gain, qkv, out, head, sems
):
    copies = []

    def store(src, dst):
        copies.append(pltpu.make_async_copy(src, dst, sems.at[len(copies)]))
        copies[-1].start()

    for n in range(4):
        at = pl.ds(n * 128, 128)
        for part, start in enumerate((QUERY, KEY, VALUE)):
            qkv[at, part * WIDTH : (part + 1) * WIDTH] = summed[at, start : start + WIDTH].astype(F32)
        store(qkv.at[at, :], g_qkv.at[at, :])
    for n in range(2):
        at = pl.ds(n * 256, 256)
        out[at, :] = mm_t(summed[at, CTX:HEAD], proj[...])
        store(out.at[at, :], g_out.at[at, :])
    head[...] = summed[:, HEAD:QUERY].astype(F32)
    store(head, g_proj)
    cols_out[...] = cols_in[...]
    g_bias[...] = summed[0:64, SMALL:PAYLOAD].astype(F32)
    small = summed[64:80, SMALL:PAYLOAD].astype(F32)
    for n in range(4):
        g_gain[:, n * LANES : (n + 1) * LANES] = small[n : n + 1]
    loss[...] = jnp.sum(small[4:5], axis=1, keepdims=True) / BATCH
    for copy in copies:
        copy.wait()


def on_device(
    atom_feats, coords, atom_counts, positives, z2, w_qkv, w_out, proj, bias_weight, ln_gain
):
    vmem = pl.BlockSpec(memory_space=pltpu.VMEM)
    smem = pl.BlockSpec(memory_space=pltpu.SMEM)
    hbm = pl.BlockSpec(memory_space=pl.ANY)
    summed, grad_z2, proj_near = pl.pallas_call(
        fused,
        out_shape=(
            pltpu.VMEM((WIDTH, PAYLOAD), BF),
            pltpu.VMEM((8, LANES), F32),
            pltpu.VMEM((WIDTH, LANES), BF),
        ),
        in_specs=[smem, smem, hbm, vmem, vmem, hbm, hbm, hbm, vmem, vmem],
        out_specs=(vmem, vmem, vmem),
        scratch_shapes=[pltpu.VMEM(*shape) for shape in SHAPES.values()]
        + [pltpu.SemaphoreType.DMA((KINDS,))] * 2
        + [pltpu.SemaphoreType.DMA((4,))],
        compiler_params=pltpu.CompilerParams(
            collective_id=0, has_side_effects=True, vmem_limit_bytes=56 * 1024 * 1024
        ),
        name="pretrain_step",
    )(
        atom_counts,
        positives,
        atom_feats.reshape(256, WIDTH),
        coords.transpose(1, 0, 2),
        z2,
        w_qkv,
        w_out,
        proj,
        bias_weight.T,
        ln_gain.reshape(1, WIDTH),
    )
    shapes = ((1, 1), (8, LANES), (WIDTH, 3 * WIDTH), (WIDTH, WIDTH), (WIDTH, LANES), (HEADS, KERNELS), (1, WIDTH))
    loss, grad_z2, g_qkv, g_out, g_proj, g_bias, g_gain = pl.pallas_call(
        unpack,
        out_shape=tuple(jax.ShapeDtypeStruct(shape, F32) for shape in shapes),
        in_specs=[vmem, vmem, vmem],
        out_specs=(vmem, vmem, hbm, hbm, hbm, vmem, vmem),
        scratch_shapes=[
            pltpu.VMEM((WIDTH, 3 * WIDTH), F32),
            pltpu.VMEM((WIDTH, WIDTH), F32),
            pltpu.VMEM((WIDTH, LANES), F32),
            pltpu.SemaphoreType.DMA((7,)),
        ],
        compiler_params=pltpu.CompilerParams(vmem_limit_bytes=32 * 1024 * 1024),
        name="unpack",
    )(summed, grad_z2, proj_near)
    return (loss.reshape(()), grad_z2, g_qkv, g_out, g_proj, g_bias.T, g_gain.reshape(WIDTH))


def solution(mesh):
    return jax.shard_map(
        on_device,
        mesh=mesh,
        in_specs=(
            P(("dp", "group"), None, None),
            P(("dp", "group"), None, None),
            P(("dp", "group")),
            P(("dp", "group")),
            P(("dp", "group"), None),
            P(),
            P(),
            P(),
            P(),
            P(),
        ),
        out_specs=(P(), P(("dp", "group"), None), P(), P(), P(), P(), P()),
        check_vma=False,
    )
```

```python
import functools

import jax
import jax.numpy as jnp
from jax import lax
from jax.experimental import pallas as pl
from jax.experimental.pallas import tpu as pltpu
from jax.sharding import PartitionSpec as P

MESH = pl.DeviceIdType.MESH
F32 = jnp.float32
BF = jnp.bfloat16

MOLS = 8
PAIRS = 4
ATOMS = 32
WIDTH = 512
HEADS = 64
HEAD_DIM = 8
KERNELS = 128
LANES = 128
WIDE = HEAD_DIM * LANES
BATCH = 2048
SIDE = 16
DEPTH = 8

VALUE, CTX, HEAD, QUERY, KEY, SMALL, PAYLOAD = 0, 512, 640, 768, 1280, 1792, 1920
CHUNKS = (((0, 384), (384, 768)), ((768, 1024), (1024, 1280)), ((1280, 1664), (1664, 1920)))

Z2, POS, Z3, ROWS, COLS, UNIT, GZ2 = range(7)
FIRST, SECOND, RING, SHARE_SECOND, SHARE_FIRST, CORE_OUT = (7 + 6 * n for n in range(6))
CORE = 43
KINDS = CORE + 3


def mm(a, b):
    return lax.dot_general(a, b, (((1,), (0,)), ((), ())), preferred_element_type=F32)


def mm_t(a, b):
    return lax.dot_general(a, b, (((1,), (1,)), ((), ())), preferred_element_type=F32)


def tmm(a, b):
    return lax.dot_general(a, b, (((0,), (0,)), ((), ())), preferred_element_type=F32)


def halves(values):
    high = values.astype(BF)
    return high, (values - high.astype(F32)).astype(BF)


def stacked(values):
    high = values.astype(BF).astype(F32)
    return jnp.concatenate([high, values - high], axis=0).astype(BF)


def two_part(values, weights, product):
    rows = values.shape[0]
    both = product(stacked(values), weights)
    return both[:rows] + both[rows:]


def lane_is_odd(shape):
    return (lax.broadcasted_iota(jnp.int32, shape, len(shape) - 1) & 64) != 0


def remote(src, dst, sems, kind, device):
    return pltpu.make_async_remote_copy(
        src_ref=src,
        dst_ref=dst,
        send_sem=sems[0].at[kind],
        recv_sem=sems[1].at[kind],
        device_id=device,
        device_id_type=MESH,
    )


def subsets(flips, start):
    places = [start]
    for flip in flips:
        places = places + [tuple(p + f for p, f in zip(place, flip)) for place in places]
    return places


def normalize(feats, counts, gain, s):
    x = feats[...].astype(F32)
    mean = jnp.mean(x, axis=-1, keepdims=True)
    centred = x - mean
    var = jnp.mean(centred * centred, axis=-1, keepdims=True)
    xhat = centred * lax.rsqrt(var + 1e-05)
    s.xhat[...] = xhat
    normed = (xhat * gain[...]).astype(BF)
    s.normed[...] = normed
    for m in range(MOLS):
        valid = lax.broadcasted_iota(jnp.int32, (ATOMS, WIDTH), 0) < counts[m]
        s.xsum[m : m + 1, :] = jnp.sum(
            jnp.where(valid, x[m * ATOMS : (m + 1) * ATOMS], 0.0), axis=0, keepdims=True
        )


def make_perm(s):
    row = lax.broadcasted_iota(jnp.int32, (WIDTH, WIDE), 0)
    col = lax.broadcasted_iota(jnp.int32, (WIDTH, WIDE), 1)
    placed = ((row >> 3) == (col & 63)) & ((row & 7) == (col >> 7))
    s.perm[...] = jnp.where(placed, 1.0, 0.0).astype(BF)


def project(wqkv, s):
    normed = s.normed[...]
    odd = lane_is_odd((ATOMS, WIDE))
    for part, (target, scale) in enumerate(((s.q, HEAD_DIM ** (-0.5)), (s.k, 1.0), (s.v, 1.0))):
        projected = mm(normed, wqkv[:, part * WIDTH : (part + 1) * WIDTH]).astype(BF)
        spread = mm(projected, s.perm[...])
        for p in range(PAIRS):
            low = spread[(2 * p) * ATOMS : (2 * p + 1) * ATOMS]
            high = spread[(2 * p + 1) * ATOMS : (2 * p + 2) * ATOMS]
            merged = jnp.where(odd, high, low)
            target[p] = merged * scale if scale != 1.0 else merged


def distances(coords, s):
    atom = lax.broadcasted_iota(jnp.int32, (ATOMS, ATOMS * ATOMS), 0)
    pair = lax.broadcasted_iota(jnp.int32, (ATOMS, ATOMS * ATOMS), 1)
    select = (
        jnp.where(atom == (pair & 31), 1.0, 0.0) - jnp.where(atom == (pair >> 5), 1.0, 0.0)
    ).astype(BF)
    squared = jnp.zeros((MOLS, ATOMS * ATOMS), F32)
    for c in range(3):
        values = coords[c]
        first = values.astype(BF).astype(F32)
        second = (values - first).astype(BF).astype(F32)
        third = values - first - second
        three = mm(jnp.concatenate([first, second, third], axis=0).astype(BF), select)
        offset = three[:MOLS] + three[MOLS : 2 * MOLS] + three[2 * MOLS :]
        squared = squared + offset * offset
    distance = jnp.sqrt(squared + 0.25)
    for m in range(MOLS):
        s.distance[m] = distance[m : m + 1]


def bias_matrix(bias_t, s):
    turned = jnp.concatenate([bias_t[...], bias_t[...]], axis=0)
    upper = lax.broadcasted_iota(jnp.int32, (LANES, KERNELS), 0) < HEADS
    blocks = jnp.concatenate([jnp.where(upper, turned, 0.0), jnp.where(upper, 0.0, turned)], axis=1)
    s.bias_lhs[...] = stacked(blocks)


def pair_biases(s):
    centers = lax.broadcasted_iota(jnp.int32, (KERNELS, 2 * LANES), 0).astype(F32) * (12.0 / KERNELS)

    def one_pair(p, carry):
        for block in range(4):
            at = pl.ds(block * 256, 256)
            basis = []
            for parity in range(2):
                away = (s.distance[2 * p + parity, :, at] - centers) * 2.0
                basis.append(jnp.exp(-(away * away)))
            high, low = halves(jnp.concatenate(basis, axis=0))
            s.basis[p, :, at] = high
            both = mm(s.bias_lhs[...], high)
            bias = both[:LANES] + both[LANES:] + mm(s.bias_lhs[:LANES, :], low)
            s.attn[p, at, :] = bias.T
        return carry

    lax.fori_loop(0, PAIRS, one_pair, 0, unroll=True)


def attend(counts, s):
    def one_pair(p, carry):
        count = jnp.where(lane_is_odd((1, LANES)), counts[2 * p + 1], counts[2 * p])
        top = jnp.full((ATOMS, LANES), -1e30, F32)
        for j in range(ATOMS):
            at = pl.ds(j * ATOMS, ATOMS)
            score = s.attn[p, at, :]
            for d in range(HEAD_DIM):
                lanes = pl.ds(d * LANES, LANES)
                score = score + s.q[p, :, lanes] * s.k[p, j : j + 1, lanes]
            score = jnp.where(j < count, score, -1e30)
            s.attn[p, at, :] = score
            top = jnp.maximum(top, score)
        total = jnp.zeros((ATOMS, LANES), F32)
        for j in range(ATOMS):
            at = pl.ds(j * ATOMS, ATOMS)
            expo = jnp.exp(s.attn[p, at, :] - top)
            s.attn[p, at, :] = expo
            total = total + expo
        real = lax.broadcasted_iota(jnp.int32, (ATOMS, LANES), 0) < count
        share = jnp.where(real, 1.0 / total, 0.0)
        for j in range(ATOMS):
            at = pl.ds(j * ATOMS, ATOMS)
            weight = s.attn[p, at, :] * share
            s.attn[p, at, :] = weight
            s.column[p, j : j + 1, :] = jnp.sum(weight, axis=0, keepdims=True)
        odd_row = lane_is_odd((1, LANES))
        for d in range(HEAD_DIM):
            lanes = pl.ds(d * LANES, LANES)
            context = jnp.sum(s.column[p] * s.v[p, :, lanes], axis=0, keepdims=True)
            s.context[2 * p, :, lanes] = jnp.where(odd_row, 0.0, context)
            s.context[2 * p + 1, :, lanes] = jnp.where(odd_row, context, 0.0)
        return carry

    lax.fori_loop(0, PAIRS, one_pair, 0)

def pool(wout, proj, s):
    context = jnp.concatenate([s.context[m] for m in range(MOLS)], axis=0)
    context = two_part(context, s.perm[...], mm_t)
    s.ctx_sum[...] = context
    pooled = (s.xsum[...] + two_part(context, wout[...], mm)).astype(BF)
    s.pooled[...] = pooled.astype(F32)
    return mm(pooled, proj[...])


def start_backward(grad_z3, wout, proj, s):
    cs_high, cs_low = halves(s.ctx_sum[...])
    g_high, g_low = halves(grad_z3)
    f = lambda v: v.astype(F32)
    left = jnp.concatenate([f(cs_high), f(cs_low), f(cs_high)], axis=0).astype(BF)
    right = jnp.concatenate([f(g_high), f(g_high), f(g_low)], axis=0).astype(BF)
    s.payload[:, CTX:HEAD] = tmm(left, right).astype(BF)
    left = jnp.concatenate([s.pooled[...], s.pooled[...]], axis=0).astype(BF)
    right = jnp.concatenate([f(g_high), f(g_low)], axis=0).astype(BF)
    s.payload[:, HEAD:QUERY] = tmm(left, right).astype(BF)

    grad_pooled = two_part(grad_z3, proj[...], mm_t)
    grad_ctx = two_part(grad_pooled, wout[...], mm_t)
    spread = two_part(grad_ctx, s.perm[...], mm)
    for m in range(MOLS):
        s.context[m] = spread[m : m + 1]


def value_backward(s):
    odd_row = lane_is_odd((1, LANES))

    def one_pair(p, carry):
        along = jnp.zeros((ATOMS, LANES), F32)
        for d in range(HEAD_DIM):
            lanes = pl.ds(d * LANES, LANES)
            grad = jnp.where(odd_row, s.context[2 * p + 1, :, lanes], s.context[2 * p, :, lanes])
            along = along + grad * s.v[p, :, lanes]
            s.dv[p, :, lanes] = (s.column[p] * grad).astype(BF)
        s.along[p] = along
        return carry

    lax.fori_loop(0, PAIRS, one_pair, 0)


def attend_backward(first, last, s):
    scale = HEAD_DIM ** (-0.5)

    def one_pair(p, carry):
        mean = jnp.zeros((ATOMS, LANES), F32)
        for j in range(ATOMS):
            mean = mean + s.attn[p, pl.ds(j * ATOMS, ATOMS), :] * s.along[p, j : j + 1, :]
        for half in range(2):
            ds_range = range(4 * half, 4 * half + 4)
            sums = [jnp.zeros((ATOMS, LANES), F32) for d in ds_range]
            for j in range(ATOMS):
                at = pl.ds(j * ATOMS, ATOMS)
                if half == 0:
                    slope = s.attn[p, at, :] * (s.along[p, j : j + 1, :] - mean)
                    s.attn[p, at, :] = slope
                else:
                    slope = s.attn[p, at, :]
                for n, d in enumerate(ds_range):
                    lanes = pl.ds(d * LANES, LANES)
                    sums[n] = sums[n] + slope * s.k[p, j : j + 1, lanes]
                    s.dk[j : j + 1, lanes] = jnp.sum(slope * s.q[p, :, lanes], axis=0, keepdims=True)
            for n, d in enumerate(ds_range):
                s.dqs[p, :, pl.ds(d * LANES, LANES)] = (sums[n] * scale).astype(BF)
        s.dks[p] = s.dk[...].astype(BF)
        return carry

    lax.fori_loop(first, last, one_pair, 0)


def bias_backward(s):
    bias_sum = jnp.zeros((2 * KERNELS, LANES), F32)
    for p in range(PAIRS):
        bias_sum = bias_sum + mm(s.basis[p], s.attn[p].astype(BF))
    odd = lane_is_odd((KERNELS, LANES))
    folded = jnp.where(odd, bias_sum[KERNELS:], bias_sum[:KERNELS]).T
    s.small[...] = jnp.zeros((WIDTH, LANES), F32)
    s.small[0:64, :] = folded[:64] + folded[64:]


def project_backward(source, part, target, s):
    odd = lane_is_odd((ATOMS, WIDE))
    zero = jnp.zeros((ATOMS, WIDE), BF)
    pieces = []
    for m in range(MOLS):
        value = source[m // 2]
        pieces.append(jnp.where(odd, value, zero) if m % 2 else jnp.where(odd, zero, value))
    dproj = mm_t(jnp.concatenate(pieces, axis=0), s.perm[...]).astype(BF)
    s.dproj[:, part * WIDTH : (part + 1) * WIDTH] = dproj
    s.payload[:, target : target + WIDTH] = tmm(s.normed[...], dproj).astype(BF)


def gain_backward(wqkv, s):
    grad_normed = mm_t(s.dproj[...], wqkv[...])
    grad_gain = jnp.sum(grad_normed * s.xhat[...], axis=0, keepdims=True)
    for n in range(4):
        s.small[64 + n : 65 + n, :] = grad_gain[:, n * LANES : (n + 1) * LANES]


def fused(
    counts,
    positives,
    feats_in,
    coords,
    z2,
    wqkv_in,
    wout_in,
    proj_in,
    bias_t,
    gain,
    summed,
    grad_z2,
    proj,
    *scratch,
):
    s = Scratch(scratch)
    sems = (s.send, s.recv)
    loads = [
        pltpu.make_async_copy(src, dst, s.load.at[n])
        for n, (src, dst) in enumerate(
            ((feats_in, s.feats), (wqkv_in, s.wqkv), (wout_in, s.wout), (proj_in, proj))
        )
    ]
    for load in loads:
        load.start()
    feats, wqkv, wout = s.feats, s.wqkv, s.wout

    dp, y_high = lax.axis_index("dp"), lax.axis_index("group")
    bits = [(dp // 2**n) % 2 for n in range(7)]
    cross = [2**n * (1 - 2 * bits[n]) for n in range(7)]
    cross_y = 1 - 2 * y_high
    core = bits[0]
    x_at = bits[1] + 2 * bits[2]
    y_at = bits[3] * 2 + y_high
    ring = dp // 16
    plane = y_high + 2 * x_at + 8 * bits[3]
    depth = core + 2 * ring
    along_row = subsets(
        ((0, cross_y, cross_y), (cross[1], 0, cross[1]), (cross[2], 0, cross[2]), (cross[3], 0, cross[3])),
        (dp, y_high, plane),
    )
    along_col = subsets(
        (
            (cross[0], 0, cross[0]),
            (cross[4], 0, 2 * (1 - 2 * bits[4])),
            (cross[5], 0, 4 * (1 - 2 * bits[5])),
            (cross[6], 0, 8 * (1 - 2 * bits[6])),
        ),
        (dp, y_high, depth),
    )
    along_x = subsets(
        ((cross[1], 0, 1 - 2 * bits[1]), (cross[2], 0, 2 * (1 - 2 * bits[2]))), (dp, y_high, x_at)
    )
    along_y = subsets(
        ((0, cross_y, cross_y), (cross[3], 0, 2 * (1 - 2 * bits[3]))), (dp, y_high, y_at)
    )
    along_ring = along_col[0::2]
    sibling = along_col[1][:2]

    barrier = pltpu.get_barrier_semaphore()
    for place in along_row[1:] + along_col[1:]:
        pl.semaphore_signal(barrier, inc=1, device_id=place[:2], device_id_type=MESH)

    loads[0].wait()
    normalize(feats, counts, gain, s)
    make_perm(s)
    loads[1].wait()
    project(wqkv, s)
    distances(coords, s)
    bias_matrix(bias_t, s)
    pair_biases(s)
    pl.semaphore_wait(barrier, 2 * (SIDE - 1))

    def slot(n):
        return pl.ds(n * 8, 8)

    others = range(1, SIDE)

    def start(copy, offsets=others):
        for o in offsets:
            copy(o).start()

    def all_of(ref, kind):
        return remote(ref, ref, sems, kind, sibling)

    def wait(ref, kind):
        all_of(ref, kind).wait()

    s.z2[slot(depth), :] = z2[...].astype(F32)
    targets = jnp.zeros((8, LANES), jnp.int32)
    sub = lax.broadcasted_iota(jnp.int32, (8, LANES), 0)
    for n in range(8):
        targets = jnp.where(sub == n, positives[n], targets)
    s.pos[slot(plane), :] = targets

    def z2_copy(o):
        mine = s.z2.at[slot(depth), :]
        return remote(mine, mine, sems, Z2, along_col[o][:2])

    def pos_copy(o):
        mine = s.pos.at[slot(plane), :]
        return remote(mine, mine, sems, POS, along_row[o][:2])

    def z3_copy(o):
        mine = s.z3.at[slot(plane), :]
        return remote(mine, mine, sems, Z3, along_row[o][:2])

    def rows_copy(o):
        mine = s.rows.at[plane]
        return remote(mine, mine, sems, ROWS, along_row[o][:2])

    def cols_copy(o):
        mine = s.cols.at[depth]
        return remote(mine, mine, sems, COLS, along_col[o][:2])

    def unit_copy(o):
        peer = along_row[o]
        return remote(s.unit.at[peer[2]], s.unit_in.at[plane], sems, UNIT, peer[:2])

    def gz2_copy(o):
        peer = along_col[o]
        return remote(s.gz2.at[peer[2]], s.gz2_in.at[depth], sems, GZ2, peer[:2])

    start(z2_copy)
    start(pos_copy)

    attend(counts, s)
    loads[2].wait()
    loads[3].wait()
    z3 = pool(wout, proj, s)
    inverse = lax.rsqrt(jnp.mean(z3 * z3, axis=1, keepdims=True) + 1e-06) * LANES ** (-0.5)
    s.z3[slot(plane), :] = (z3 * inverse).astype(BF).astype(F32)
    start(z3_copy)
    wait(s.z2.at[pl.ds(0, 120), :], Z2)
    wait(s.pos.at[pl.ds(0, 120), :], POS)
    wait(s.z3.at[pl.ds(0, 120), :], Z3)

    z3_all = s.z3[...].astype(BF)
    z2_all = s.z2[...].astype(BF)
    logits = mm_t(z3_all, z2_all)
    expo = jnp.exp(logits)
    expo_t = jnp.exp(mm_t(z2_all, z3_all))
    s.rows[plane] = jnp.sum(expo_t, axis=0, keepdims=True)
    s.cols[depth] = jnp.sum(expo, axis=0, keepdims=True)
    start(rows_copy)
    start(cols_copy)
    lane = lax.broadcasted_iota(jnp.int32, (LANES, LANES), 1)
    owner = (lane >> 4) * 32 + ((lane >> 3) & 1) * 2 + (dp * 2 + y_high - ring * 32 - core * 2)
    column_id = owner * 8 + (lane & 7)
    hit = s.pos[...] == column_id
    score = jnp.sum(jnp.where(hit, logits, 0.0), axis=0, keepdims=True)
    wait(s.rows.at[pl.ds(0, 15)], ROWS)
    wait(s.cols.at[pl.ds(0, 15)], COLS)
    row_sum = s.rows[0]
    col_sum = s.cols[0]
    for n in range(1, SIDE):
        row_sum = row_sum + s.rows[n]
        col_sum = col_sum + s.cols[n]
    row_half = jnp.broadcast_to(0.5 / row_sum, (LANES, LANES)).T
    slope = expo * (row_half + 0.5 / col_sum) - jnp.where(hit, 1.0, 0.0)
    unit = mm(slope.astype(BF), z2_all)
    for n in range(SIDE):
        s.unit[n] = unit[n * 8 : (n + 1) * 8]
    s.unit_in[plane] = s.unit[plane]
    start(unit_copy)
    grad_cols = tmm(slope.astype(BF), z3_all)
    for n in range(SIDE):
        s.gz2[n] = grad_cols[n * 8 : (n + 1) * 8]
    s.gz2_in[depth] = s.gz2[depth]
    start(gz2_copy)
    one_lane = lax.broadcasted_iota(jnp.int32, (1, LANES), 1)
    row_term = jnp.where((one_lane >> 3) == plane, 0.5 * jnp.log(row_sum), 0.0)
    col_term = jnp.where((one_lane >> 3) == depth, 0.5 * jnp.log(col_sum), 0.0)
    loss_terms = row_term + col_term - score

    wait(s.unit_in.at[pl.ds(0, 15)], UNIT)
    grad_unit = s.unit_in[0]
    for n in range(1, SIDE):
        grad_unit = grad_unit + s.unit_in[n]
    dot = jnp.sum(z3 * grad_unit, axis=1, keepdims=True)
    grad_z3 = inverse * (grad_unit - z3 * dot * (inverse * inverse))

    ways = ((along_x, x_at, along_y, y_at), (along_y, y_at, along_x, x_at))

    def lanes_of(c, h):
        return pl.ds(CHUNKS[c][h][0], CHUNKS[c][h][1] - CHUNKS[c][h][0])

    def whole(c):
        return pl.ds(CHUNKS[c][0][0], CHUNKS[c][1][1] - CHUNKS[c][0][0])

    def core_copy(c):
        theirs = s.payload.at[pl.ds((1 - core) * 256, 256), whole(c)]
        return remote(theirs, s.core_in.at[:, whole(c)], sems, CORE + c, sibling)

    def first_copy(c, h, o):
        peer, lanes = ways[h][0][o], lanes_of(c, h)
        return remote(
            s.first_out.at[pl.ds(peer[2] * 64, 64), lanes],
            s.first_in.at[ways[h][1], :, lanes],
            sems,
            FIRST + 2 * c + h,
            peer[:2],
        )

    def second_copy(c, h, o):
        peer, lanes = ways[h][2][o], lanes_of(c, h)
        return remote(
            s.second_out.at[pl.ds(peer[2] * 16, 16), lanes],
            s.second_in.at[ways[h][3], :, lanes],
            sems,
            SECOND + 2 * c + h,
            peer[:2],
        )

    def ring_copy(c, h, o):
        lanes = lanes_of(c, h)
        return remote(
            s.ring_out.at[:, lanes],
            s.ring_in.at[ring, :, lanes],
            sems,
            RING + 2 * c + h,
            along_ring[o][:2],
        )

    def second_share(c, h, o):
        mine = summed.at[pl.ds(core * 256 + ways[h][1] * 64 + ways[h][3] * 16, 16), lanes_of(c, h)]
        return remote(mine, mine, sems, SHARE_SECOND + 2 * c + h, ways[h][2][o][:2])

    def first_share(c, h, o):
        mine = summed.at[pl.ds(core * 256 + ways[h][1] * 64, 64), lanes_of(c, h)]
        return remote(mine, mine, sems, SHARE_FIRST + 2 * c + h, ways[h][0][o][:2])

    def core_share(c, h):
        mine = summed.at[pl.ds(core * 256, 256), lanes_of(c, h)]
        return remote(mine, mine, sems, CORE_OUT + 2 * c + h, sibling)

    near, far = range(1, 4), range(1, DEPTH)

    def all_first(c, h):
        return all_of(s.first_in.at[pl.ds(0, 3), :, lanes_of(c, h)], FIRST + 2 * c + h)

    def all_second(c, h):
        return all_of(s.second_in.at[pl.ds(0, 3), :, lanes_of(c, h)], SECOND + 2 * c + h)

    def all_ring(c, h):
        return all_of(s.ring_in.at[pl.ds(0, 7), :, lanes_of(c, h)], RING + 2 * c + h)

    def all_second_share(c, h):
        return all_of(s.second_in.at[pl.ds(0, 3), :, lanes_of(c, h)], SHARE_SECOND + 2 * c + h)

    def all_first_share(c, h):
        return all_of(s.first_in.at[pl.ds(0, 3), :, lanes_of(c, h)], SHARE_FIRST + 2 * c + h)

    def added(ref, count, lanes):
        total = ref[0, :, lanes].astype(F32)
        for n in range(1, count):
            total = total + ref[n, :, lanes].astype(F32)
        return total.astype(BF)

    def first_step(c):
        core_copy(c).wait_recv()
        mine = s.payload[pl.ds(core * 256, 256), whole(c)].astype(F32)
        s.first_out[:, whole(c)] = (mine + s.core_in[:, whole(c)].astype(F32)).astype(BF)
        for h in range(2):
            for o in near:
                first_copy(c, h, o).start()
        for h in range(2):
            lanes, at = lanes_of(c, h), ways[h][1]
            s.first_in[at, :, lanes] = s.first_out[pl.ds(at * 64, 64), lanes]

    def second_step(c):
        for h in range(2):
            lanes, at = lanes_of(c, h), ways[h][3]
            all_first(c, h).wait_recv()
            s.second_out[:, lanes] = added(s.first_in, 4, lanes)
            for o in near:
                second_copy(c, h, o).start()
            s.second_in[at, :, lanes] = s.second_out[pl.ds(at * 16, 16), lanes]

    def ring_step(c):
        for h in range(2):
            lanes = lanes_of(c, h)
            all_second(c, h).wait_recv()
            total = added(s.second_in, 4, lanes)
            s.ring_out[:, lanes] = total
            for o in far:
                ring_copy(c, h, o).start()
            s.ring_in[ring, :, lanes] = total

    def share_second_step(c):
        for h in range(2):
            lanes = lanes_of(c, h)
            all_ring(c, h).wait_recv()
            at = pl.ds(core * 256 + ways[h][1] * 64 + ways[h][3] * 16, 16)
            summed[at, lanes] = added(s.ring_in, DEPTH, lanes)
            for o in near:
                second_share(c, h, o).start()

    def share_first_step(c):
        for h in range(2):
            all_second_share(c, h).wait_recv()
            for o in near:
                first_share(c, h, o).start()

    def share_core_step(c):
        for h in range(2):
            all_first_share(c, h).wait_recv()
            core_share(c, h).start()

    def arrive_step(c):
        for h in range(2):
            core_share(c, h).wait_recv()

    start_backward(grad_z3, wout, proj, s)
    value_backward(s)
    project_backward(s.dv, 2, VALUE, s)
    core_copy(0).start()
    attend_backward(0, 2, s)
    first_step(0)
    attend_backward(2, PAIRS, s)
    project_backward(s.dqs, 0, QUERY, s)
    core_copy(1).start()
    project_backward(s.dks, 1, KEY, s)
    first_step(1)
    bias_backward(s)
    gain_backward(wqkv, s)
    s.small[68:69, :] = loss_terms
    s.payload[:, SMALL:PAYLOAD] = s.small[...].astype(BF)
    core_copy(2).start()
    second_step(0)
    first_step(2)
    ring_step(0)
    second_step(1)
    second_step(2)
    ring_step(1)
    ring_step(2)
    share_second_step(0)
    share_first_step(0)
    share_second_step(1)
    share_second_step(2)
    share_first_step(1)
    share_core_step(0)
    share_first_step(2)
    share_core_step(1)
    arrive_step(0)
    share_core_step(2)
    arrive_step(1)

    wait(s.gz2_in.at[pl.ds(0, 15)], GZ2)
    total = s.gz2_in[0]
    for n in range(1, SIDE):
        total = total + s.gz2_in[n]
    grad_z2[...] = total
    arrive_step(2)
    for c in range(3):
        core_copy(c).wait_send()
        for h in range(2):
            for group in (all_first, all_second, all_ring, all_second_share, all_first_share):
                group(c, h).wait_send()
            core_share(c, h).wait_send()


SHAPES = {
    "xhat": ((256, WIDTH), F32),
    "normed": ((256, WIDTH), BF),
    "xsum": ((MOLS, WIDTH), F32),
    "perm": ((WIDTH, WIDE), BF),
    "q": ((PAIRS, ATOMS, WIDE), F32),
    "k": ((PAIRS, ATOMS, WIDE), F32),
    "v": ((PAIRS, ATOMS, WIDE), F32),
    "distance": ((MOLS, 1, ATOMS * ATOMS), F32),
    "bias_lhs": ((2 * LANES, 2 * KERNELS), BF),
    "basis": ((PAIRS, 2 * KERNELS, ATOMS * ATOMS), BF),
    "attn": ((PAIRS, ATOMS * ATOMS, LANES), F32),
    "column": ((PAIRS, ATOMS, LANES), F32),
    "context": ((MOLS, 1, WIDE), F32),
    "ctx_sum": ((MOLS, WIDTH), F32),
    "pooled": ((MOLS, WIDTH), F32),
    "along": ((PAIRS, ATOMS, LANES), F32),
    "dk": ((ATOMS, WIDE), F32),
    "dqs": ((PAIRS, ATOMS, WIDE), BF),
    "dks": ((PAIRS, ATOMS, WIDE), BF),
    "dv": ((PAIRS, ATOMS, WIDE), BF),
    "dproj": ((256, 3 * WIDTH), BF),
    "small": ((WIDTH, LANES), F32),
    "payload": ((WIDTH, PAYLOAD), BF),
    "z2": ((LANES, LANES), F32),
    "pos": ((LANES, LANES), jnp.int32),
    "z3": ((LANES, LANES), F32),
    "rows": ((SIDE, 1, LANES), F32),
    "cols": ((SIDE, 1, LANES), F32),
    "unit": ((SIDE, 8, LANES), F32),
    "unit_in": ((SIDE, 8, LANES), F32),
    "gz2": ((SIDE, 8, LANES), F32),
    "gz2_in": ((SIDE, 8, LANES), F32),
    "core_in": ((256, PAYLOAD), BF),
    "first_out": ((256, PAYLOAD), BF),
    "first_in": ((4, 64, PAYLOAD), BF),
    "second_out": ((64, PAYLOAD), BF),
    "second_in": ((4, 16, PAYLOAD), BF),
    "ring_out": ((16, PAYLOAD), BF),
    "ring_in": ((DEPTH, 16, PAYLOAD), BF),
    "feats": ((256, WIDTH), BF),
    "wqkv": ((WIDTH, 3 * WIDTH), BF),
    "wout": ((WIDTH, WIDTH), BF),
}


class Scratch:
    def __init__(self, refs):
        for name, ref in zip(list(SHAPES) + ["send", "recv", "load"], refs):
            setattr(self, name, ref)


def unpack(
    summed, cols_in, proj, loss, cols_out, g_qkv, g_out, g_proj, g_bias, g_gain, qkv, out, head, sems
):
    copies = []

    def store(src, dst):
        copies.append(pltpu.make_async_copy(src, dst, sems.at[len(copies)]))
        copies[-1].start()

    for n in range(4):
        at = pl.ds(n * 128, 128)
        for part, start in enumerate((QUERY, KEY, VALUE)):
            qkv[at, part * WIDTH : (part + 1) * WIDTH] = summed[at, start : start + WIDTH].astype(F32)
        store(qkv.at[at, :], g_qkv.at[at, :])
    for n in range(2):
        at = pl.ds(n * 256, 256)
        out[at, :] = mm_t(summed[at, CTX:HEAD], proj[...])
        store(out.at[at, :], g_out.at[at, :])
    head[...] = summed[:, HEAD:QUERY].astype(F32)
    store(head, g_proj)
    cols_out[...] = cols_in[...]
    g_bias[...] = summed[0:64, SMALL:PAYLOAD].astype(F32)
    small = summed[64:80, SMALL:PAYLOAD].astype(F32)
    for n in range(4):
        g_gain[:, n * LANES : (n + 1) * LANES] = small[n : n + 1]
    loss[...] = jnp.sum(small[4:5], axis=1, keepdims=True) / BATCH
    for copy in copies:
        copy.wait()


def on_device(
    atom_feats, coords, atom_counts, positives, z2, w_qkv, w_out, proj, bias_weight, ln_gain
):
    vmem = pl.BlockSpec(memory_space=pltpu.VMEM)
    smem = pl.BlockSpec(memory_space=pltpu.SMEM)
    hbm = pl.BlockSpec(memory_space=pl.ANY)
    summed, grad_z2, proj_near = pl.pallas_call(
        fused,
        out_shape=(
            pltpu.VMEM((WIDTH, PAYLOAD), BF),
            pltpu.VMEM((8, LANES), F32),
            pltpu.VMEM((WIDTH, LANES), BF),
        ),
        in_specs=[smem, smem, hbm, vmem, vmem, hbm, hbm, hbm, vmem, vmem],
        out_specs=(vmem, vmem, vmem),
        scratch_shapes=[pltpu.VMEM(*shape) for shape in SHAPES.values()]
        + [pltpu.SemaphoreType.DMA((KINDS,))] * 2
        + [pltpu.SemaphoreType.DMA((4,))],
        compiler_params=pltpu.CompilerParams(
            collective_id=0, has_side_effects=True, vmem_limit_bytes=56 * 1024 * 1024
        ),
        name="pretrain_step",
    )(
        atom_counts,
        positives,
        atom_feats.reshape(256, WIDTH),
        coords.transpose(1, 0, 2),
        z2,
        w_qkv,
        w_out,
        proj,
        bias_weight.T,
        ln_gain.reshape(1, WIDTH),
    )
    shapes = ((1, 1), (8, LANES), (WIDTH, 3 * WIDTH), (WIDTH, WIDTH), (WIDTH, LANES), (HEADS, KERNELS), (1, WIDTH))
    loss, grad_z2, g_qkv, g_out, g_proj, g_bias, g_gain = pl.pallas_call(
        unpack,
        out_shape=tuple(jax.ShapeDtypeStruct(shape, F32) for shape in shapes),
        in_specs=[vmem, vmem, vmem],
        out_specs=(vmem, vmem, hbm, hbm, hbm, vmem, vmem),
        scratch_shapes=[
            pltpu.VMEM((WIDTH, 3 * WIDTH), F32),
            pltpu.VMEM((WIDTH, WIDTH), F32),
            pltpu.VMEM((WIDTH, LANES), F32),
            pltpu.SemaphoreType.DMA((7,)),
        ],
        compiler_params=pltpu.CompilerParams(vmem_limit_bytes=32 * 1024 * 1024),
        name="unpack",
    )(summed, grad_z2, proj_near)
    return (loss.reshape(()), grad_z2, g_qkv, g_out, g_proj, g_bias.T, g_gain.reshape(WIDTH))


def solution(mesh):
    return jax.shard_map(
        on_device,
        mesh=mesh,
        in_specs=(
            P(("dp", "group"), None, None),
            P(("dp", "group"), None, None),
            P(("dp", "group")),
            P(("dp", "group")),
            P(("dp", "group"), None),
            P(),
            P(),
            P(),
            P(),
            P(),
        ),
        out_specs=(P(), P(("dp", "group"), None), P(), P(), P(), P(), P()),
        check_vma=False,
    )
```

```python
import functools

import jax
import jax.numpy as jnp
from jax import lax
from jax.experimental import pallas as pl
from jax.experimental.pallas import tpu as pltpu
from jax.sharding import PartitionSpec as P

MESH = pl.DeviceIdType.MESH
F32 = jnp.float32
BF = jnp.bfloat16

MOLS = 8
PAIRS = 4
ATOMS = 32
WIDTH = 512
HEADS = 64
HEAD_DIM = 8
KERNELS = 128
LANES = 128
WIDE = HEAD_DIM * LANES
BATCH = 2048
SIDE = 16
DEPTH = 8

VALUE, CTX, HEAD, QUERY, KEY, SMALL, PAYLOAD = 0, 512, 640, 768, 1280, 1792, 1920
CHUNKS = (((0, 384), (384, 768)), ((768, 1024), (1024, 1280)), ((1280, 1664), (1664, 1920)))

Z2, POS, Z3, ROWS, COLS, UNIT, GZ2 = range(7)
FIRST, SECOND, RING, SHARE_SECOND, SHARE_FIRST, CORE_OUT = (7 + 6 * n for n in range(6))
CORE = 43
KINDS = CORE + 3


def mm(a, b):
    return lax.dot_general(a, b, (((1,), (0,)), ((), ())), preferred_element_type=F32)


def mm_t(a, b):
    return lax.dot_general(a, b, (((1,), (1,)), ((), ())), preferred_element_type=F32)


def tmm(a, b):
    return lax.dot_general(a, b, (((0,), (0,)), ((), ())), preferred_element_type=F32)


def halves(values):
    high = values.astype(BF)
    return high, (values - high.astype(F32)).astype(BF)


def stacked(values):
    high = values.astype(BF).astype(F32)
    return jnp.concatenate([high, values - high], axis=0).astype(BF)


def two_part(values, weights, product):
    rows = values.shape[0]
    both = product(stacked(values), weights)
    return both[:rows] + both[rows:]


def lane_is_odd(shape):
    return (lax.broadcasted_iota(jnp.int32, shape, len(shape) - 1) & 64) != 0


def remote(src, dst, sems, kind, device):
    return pltpu.make_async_remote_copy(
        src_ref=src,
        dst_ref=dst,
        send_sem=sems[0].at[kind],
        recv_sem=sems[1].at[kind],
        device_id=device,
        device_id_type=MESH,
    )


def subsets(flips, start):
    places = [start]
    for flip in flips:
        places = places + [tuple(p + f for p, f in zip(place, flip)) for place in places]
    return places


def normalize(feats, counts, gain, s):
    x = feats[...].astype(F32)
    mean = jnp.mean(x, axis=-1, keepdims=True)
    centred = x - mean
    var = jnp.mean(centred * centred, axis=-1, keepdims=True)
    xhat = centred * lax.rsqrt(var + 1e-05)
    s.xhat[...] = xhat
    normed = (xhat * gain[...]).astype(BF)
    s.normed[...] = normed
    for m in range(MOLS):
        valid = lax.broadcasted_iota(jnp.int32, (ATOMS, WIDTH), 0) < counts[m]
        s.xsum[m : m + 1, :] = jnp.sum(
            jnp.where(valid, x[m * ATOMS : (m + 1) * ATOMS], 0.0), axis=0, keepdims=True
        )


def make_perm(s):
    row = lax.broadcasted_iota(jnp.int32, (WIDTH, WIDE), 0)
    col = lax.broadcasted_iota(jnp.int32, (WIDTH, WIDE), 1)
    placed = ((row >> 3) == (col & 63)) & ((row & 7) == (col >> 7))
    s.perm[...] = jnp.where(placed, 1.0, 0.0).astype(BF)


def project(wqkv, s):
    normed = s.normed[...]
    odd = lane_is_odd((ATOMS, WIDE))
    for part, (target, scale) in enumerate(((s.q, HEAD_DIM ** (-0.5)), (s.k, 1.0), (s.v, 1.0))):
        projected = mm(normed, wqkv[:, part * WIDTH : (part + 1) * WIDTH]).astype(BF)
        spread = mm(projected, s.perm[...])
        for p in range(PAIRS):
            low = spread[(2 * p) * ATOMS : (2 * p + 1) * ATOMS]
            high = spread[(2 * p + 1) * ATOMS : (2 * p + 2) * ATOMS]
            merged = jnp.where(odd, high, low)
            target[p] = merged * scale if scale != 1.0 else merged


def distances(coords, s):
    atom = lax.broadcasted_iota(jnp.int32, (ATOMS, ATOMS * ATOMS), 0)
    pair = lax.broadcasted_iota(jnp.int32, (ATOMS, ATOMS * ATOMS), 1)
    select = (
        jnp.where(atom == (pair & 31), 1.0, 0.0) - jnp.where(atom == (pair >> 5), 1.0, 0.0)
    ).astype(BF)
    squared = jnp.zeros((MOLS, ATOMS * ATOMS), F32)
    for c in range(3):
        values = coords[c]
        first = values.astype(BF).astype(F32)
        second = (values - first).astype(BF).astype(F32)
        third = values - first - second
        three = mm(jnp.concatenate([first, second, third], axis=0).astype(BF), select)
        offset = three[:MOLS] + three[MOLS : 2 * MOLS] + three[2 * MOLS :]
        squared = squared + offset * offset
    distance = jnp.sqrt(squared + 0.25)
    for m in range(MOLS):
        s.distance[m] = distance[m : m + 1]


def bias_matrix(bias_t, s):
    turned = jnp.concatenate([bias_t[...], bias_t[...]], axis=0)
    upper = lax.broadcasted_iota(jnp.int32, (LANES, KERNELS), 0) < HEADS
    blocks = jnp.concatenate([jnp.where(upper, turned, 0.0), jnp.where(upper, 0.0, turned)], axis=1)
    s.bias_lhs[...] = stacked(blocks)


def pair_biases(s):
    centers = lax.broadcasted_iota(jnp.int32, (KERNELS, 2 * LANES), 0).astype(F32) * (12.0 / KERNELS)

    def one_pair(p, carry):
        for block in range(4):
            at = pl.ds(block * 256, 256)
            basis = []
            for parity in range(2):
                away = (s.distance[2 * p + parity, :, at] - centers) * 2.0
                basis.append(jnp.exp(-(away * away)))
            high, low = halves(jnp.concatenate(basis, axis=0))
            s.basis[p, :, at] = high
            both = mm(s.bias_lhs[...], high)
            bias = both[:LANES] + both[LANES:] + mm(s.bias_lhs[:LANES, :], low)
            s.attn[p, at, :] = bias.T
        return carry

    lax.fori_loop(0, PAIRS, one_pair, 0, unroll=True)


def attend(counts, s):
    def one_pair(p, carry):
        count = jnp.where(lane_is_odd((1, LANES)), counts[2 * p + 1], counts[2 * p])
        top = jnp.full((ATOMS, LANES), -1e30, F32)
        for j in range(ATOMS):
            at = pl.ds(j * ATOMS, ATOMS)
            score = s.attn[p, at, :]
            for d in range(HEAD_DIM):
                lanes = pl.ds(d * LANES, LANES)
                score = score + s.q[p, :, lanes] * s.k[p, j : j + 1, lanes]
            score = jnp.where(j < count, score, -1e30)
            s.attn[p, at, :] = score
            top = jnp.maximum(top, score)
        total = jnp.zeros((ATOMS, LANES), F32)
        for j in range(ATOMS):
            at = pl.ds(j * ATOMS, ATOMS)
            expo = jnp.exp(s.attn[p, at, :] - top)
            s.attn[p, at, :] = expo
            total = total + expo
        real = lax.broadcasted_iota(jnp.int32, (ATOMS, LANES), 0) < count
        share = jnp.where(real, 1.0 / total, 0.0)
        for j in range(ATOMS):
            at = pl.ds(j * ATOMS, ATOMS)
            weight = s.attn[p, at, :] * share
            s.attn[p, at, :] = weight
            s.column[p, j : j + 1, :] = jnp.sum(weight, axis=0, keepdims=True)
        odd_row = lane_is_odd((1, LANES))
        for d in range(HEAD_DIM):
            lanes = pl.ds(d * LANES, LANES)
            context = jnp.sum(s.column[p] * s.v[p, :, lanes], axis=0, keepdims=True)
            s.context[2 * p, :, lanes] = jnp.where(odd_row, 0.0, context)
            s.context[2 * p + 1, :, lanes] = jnp.where(odd_row, context, 0.0)
        return carry

    lax.fori_loop(0, PAIRS, one_pair, 0)

def pool(wout, proj, s):
    context = jnp.concatenate([s.context[m] for m in range(MOLS)], axis=0)
    context = two_part(context, s.perm[...], mm_t)
    s.ctx_sum[...] = context
    pooled = (s.xsum[...] + two_part(context, wout[...], mm)).astype(BF)
    s.pooled[...] = pooled.astype(F32)
    return mm(pooled, proj[...])


def start_backward(grad_z3, wout, proj, s):
    cs_high, cs_low = halves(s.ctx_sum[...])
    g_high, g_low = halves(grad_z3)
    f = lambda v: v.astype(F32)
    left = jnp.concatenate([f(cs_high), f(cs_low), f(cs_high)], axis=0).astype(BF)
    right = jnp.concatenate([f(g_high), f(g_high), f(g_low)], axis=0).astype(BF)
    s.payload[:, CTX:HEAD] = tmm(left, right).astype(BF)
    left = jnp.concatenate([s.pooled[...], s.pooled[...]], axis=0).astype(BF)
    right = jnp.concatenate([f(g_high), f(g_low)], axis=0).astype(BF)
    s.payload[:, HEAD:QUERY] = tmm(left, right).astype(BF)

    grad_pooled = two_part(grad_z3, proj[...], mm_t)
    grad_ctx = two_part(grad_pooled, wout[...], mm_t)
    spread = two_part(grad_ctx, s.perm[...], mm)
    for m in range(MOLS):
        s.context[m] = spread[m : m + 1]


def value_backward(s):
    odd_row = lane_is_odd((1, LANES))

    def one_pair(p, carry):
        along = jnp.zeros((ATOMS, LANES), F32)
        for d in range(HEAD_DIM):
            lanes = pl.ds(d * LANES, LANES)
            grad = jnp.where(odd_row, s.context[2 * p + 1, :, lanes], s.context[2 * p, :, lanes])
            along = along + grad * s.v[p, :, lanes]
            s.dv[p, :, lanes] = (s.column[p] * grad).astype(BF)
        s.along[p] = along
        return carry

    lax.fori_loop(0, PAIRS, one_pair, 0)


def attend_backward(first, last, s):
    scale = HEAD_DIM ** (-0.5)

    def one_pair(p, carry):
        mean = jnp.zeros((ATOMS, LANES), F32)
        for j in range(ATOMS):
            mean = mean + s.attn[p, pl.ds(j * ATOMS, ATOMS), :] * s.along[p, j : j + 1, :]
        for half in range(2):
            ds_range = range(4 * half, 4 * half + 4)
            sums = [jnp.zeros((ATOMS, LANES), F32) for d in ds_range]
            for j in range(ATOMS):
                at = pl.ds(j * ATOMS, ATOMS)
                if half == 0:
                    slope = s.attn[p, at, :] * (s.along[p, j : j + 1, :] - mean)
                    s.attn[p, at, :] = slope
                else:
                    slope = s.attn[p, at, :]
                for n, d in enumerate(ds_range):
                    lanes = pl.ds(d * LANES, LANES)
                    sums[n] = sums[n] + slope * s.k[p, j : j + 1, lanes]
                    s.dk[j : j + 1, lanes] = jnp.sum(slope * s.q[p, :, lanes], axis=0, keepdims=True)
            for n, d in enumerate(ds_range):
                s.dqs[p, :, pl.ds(d * LANES, LANES)] = (sums[n] * scale).astype(BF)
        s.dks[p] = s.dk[...].astype(BF)
        s.bias_sum[...] = s.bias_sum[...] + mm(s.basis[p], s.attn[p].astype(BF))
        return carry

    if first == 0:
        s.bias_sum[...] = jnp.zeros((2 * KERNELS, LANES), F32)

    lax.fori_loop(first, last, one_pair, 0)


def bias_backward(s):
    bias_sum = s.bias_sum[...]
    odd = lane_is_odd((KERNELS, LANES))
    folded = jnp.where(odd, bias_sum[KERNELS:], bias_sum[:KERNELS]).T
    s.small[...] = jnp.zeros((WIDTH, LANES), F32)
    s.small[0:64, :] = folded[:64] + folded[64:]


def project_backward(source, part, target, s):
    odd = lane_is_odd((ATOMS, WIDE))
    zero = jnp.zeros((ATOMS, WIDE), BF)
    pieces = []
    for m in range(MOLS):
        value = source[m // 2]
        pieces.append(jnp.where(odd, value, zero) if m % 2 else jnp.where(odd, zero, value))
    dproj = mm_t(jnp.concatenate(pieces, axis=0), s.perm[...]).astype(BF)
    s.dproj[:, part * WIDTH : (part + 1) * WIDTH] = dproj
    s.payload[:, target : target + WIDTH] = tmm(s.normed[...], dproj).astype(BF)


def gain_backward(wqkv, s):
    grad_normed = mm_t(s.dproj[...], wqkv[...])
    grad_gain = jnp.sum(grad_normed * s.xhat[...], axis=0, keepdims=True)
    for n in range(4):
        s.small[64 + n : 65 + n, :] = grad_gain[:, n * LANES : (n + 1) * LANES]


def fused(
    counts,
    positives,
    feats_in,
    coords,
    z2,
    wqkv_in,
    wout_in,
    proj_in,
    bias_t,
    gain,
    qkv,
    out,
    head,
    small,
    grad_z2,
    *scratch,
):
    s = Scratch(scratch)
    sems = (s.send, s.recv)
    loads = [
        pltpu.make_async_copy(src, dst, s.load.at[n])
        for n, (src, dst) in enumerate(
            ((feats_in, s.feats), (wqkv_in, s.wqkv), (wout_in, s.wout), (proj_in, s.proj))
        )
    ]
    for load in loads:
        load.start()
    feats, wqkv, wout, proj, summed = s.feats, s.wqkv, s.wout, s.proj, s.summed

    dp, y_high = lax.axis_index("dp"), lax.axis_index("group")
    bits = [(dp // 2**n) % 2 for n in range(7)]
    cross = [2**n * (1 - 2 * bits[n]) for n in range(7)]
    cross_y = 1 - 2 * y_high
    core = bits[0]
    x_at = bits[1] + 2 * bits[2]
    y_at = bits[3] * 2 + y_high
    ring = dp // 16
    plane = y_high + 2 * x_at + 8 * bits[3]
    depth = core + 2 * ring
    along_row = subsets(
        ((0, cross_y, cross_y), (cross[1], 0, cross[1]), (cross[2], 0, cross[2]), (cross[3], 0, cross[3])),
        (dp, y_high, plane),
    )
    along_col = subsets(
        (
            (cross[0], 0, cross[0]),
            (cross[4], 0, 2 * (1 - 2 * bits[4])),
            (cross[5], 0, 4 * (1 - 2 * bits[5])),
            (cross[6], 0, 8 * (1 - 2 * bits[6])),
        ),
        (dp, y_high, depth),
    )
    along_x = subsets(
        ((cross[1], 0, 1 - 2 * bits[1]), (cross[2], 0, 2 * (1 - 2 * bits[2]))), (dp, y_high, x_at)
    )
    along_y = subsets(
        ((0, cross_y, cross_y), (cross[3], 0, 2 * (1 - 2 * bits[3]))), (dp, y_high, y_at)
    )
    along_ring = along_col[0::2]
    sibling = along_col[1][:2]

    barrier = pltpu.get_barrier_semaphore()
    for place in along_row[1:] + along_col[1:]:
        pl.semaphore_signal(barrier, inc=1, device_id=place[:2], device_id_type=MESH)

    loads[0].wait()
    normalize(feats, counts, gain, s)
    make_perm(s)
    loads[1].wait()
    project(wqkv, s)
    distances(coords, s)
    bias_matrix(bias_t, s)
    pair_biases(s)
    pl.semaphore_wait(barrier, 2 * (SIDE - 1))

    def slot(n):
        return pl.ds(n * 8, 8)

    others = range(1, SIDE)

    def start(copy, offsets=others):
        for o in offsets:
            copy(o).start()

    def all_of(ref, kind):
        return remote(ref, ref, sems, kind, sibling)

    def wait(ref, kind):
        all_of(ref, kind).wait()

    s.z2[slot(depth), :] = z2[...].astype(F32)
    targets = jnp.zeros((8, LANES), jnp.int32)
    sub = lax.broadcasted_iota(jnp.int32, (8, LANES), 0)
    for n in range(8):
        targets = jnp.where(sub == n, positives[n], targets)
    s.pos[slot(plane), :] = targets

    def z2_copy(o):
        mine = s.z2.at[slot(depth), :]
        return remote(mine, mine, sems, Z2, along_col[o][:2])

    def pos_copy(o):
        mine = s.pos.at[slot(plane), :]
        return remote(mine, mine, sems, POS, along_row[o][:2])

    def z3_copy(o):
        mine = s.z3.at[slot(plane), :]
        return remote(mine, mine, sems, Z3, along_row[o][:2])

    def rows_copy(o):
        mine = s.rows.at[plane]
        return remote(mine, mine, sems, ROWS, along_row[o][:2])

    def cols_copy(o):
        mine = s.cols.at[depth]
        return remote(mine, mine, sems, COLS, along_col[o][:2])

    def unit_copy(o):
        peer = along_row[o]
        return remote(s.unit.at[peer[2]], s.unit_in.at[plane], sems, UNIT, peer[:2])

    def gz2_copy(o):
        peer = along_col[o]
        return remote(s.gz2.at[peer[2]], s.gz2_in.at[depth], sems, GZ2, peer[:2])

    start(z2_copy)
    start(pos_copy)

    attend(counts, s)
    loads[2].wait()
    loads[3].wait()
    z3 = pool(wout, proj, s)
    inverse = lax.rsqrt(jnp.mean(z3 * z3, axis=1, keepdims=True) + 1e-06) * LANES ** (-0.5)
    s.z3[slot(plane), :] = (z3 * inverse).astype(BF).astype(F32)
    start(z3_copy)
    wait(s.z2.at[pl.ds(0, 120), :], Z2)
    wait(s.pos.at[pl.ds(0, 120), :], POS)
    wait(s.z3.at[pl.ds(0, 120), :], Z3)

    z3_all = s.z3[...].astype(BF)
    z2_all = s.z2[...].astype(BF)
    logits = mm_t(z3_all, z2_all)
    expo = jnp.exp(logits)
    expo_t = jnp.exp(mm_t(z2_all, z3_all))
    s.rows[plane] = jnp.sum(expo_t, axis=0, keepdims=True)
    s.cols[depth] = jnp.sum(expo, axis=0, keepdims=True)
    start(rows_copy)
    start(cols_copy)
    lane = lax.broadcasted_iota(jnp.int32, (LANES, LANES), 1)
    owner = (lane >> 4) * 32 + ((lane >> 3) & 1) * 2 + (dp * 2 + y_high - ring * 32 - core * 2)
    column_id = owner * 8 + (lane & 7)
    hit = s.pos[...] == column_id
    score = jnp.sum(jnp.where(hit, logits, 0.0), axis=0, keepdims=True)
    wait(s.rows.at[pl.ds(0, 15)], ROWS)
    wait(s.cols.at[pl.ds(0, 15)], COLS)
    row_sum = s.rows[0]
    col_sum = s.cols[0]
    for n in range(1, SIDE):
        row_sum = row_sum + s.rows[n]
        col_sum = col_sum + s.cols[n]
    row_half = jnp.broadcast_to(0.5 / row_sum, (LANES, LANES)).T
    slope = expo * (row_half + 0.5 / col_sum) - jnp.where(hit, 1.0, 0.0)
    unit = mm(slope.astype(BF), z2_all)
    for n in range(SIDE):
        s.unit[n] = unit[n * 8 : (n + 1) * 8]
    s.unit_in[plane] = s.unit[plane]
    start(unit_copy)
    grad_cols = tmm(slope.astype(BF), z3_all)
    for n in range(SIDE):
        s.gz2[n] = grad_cols[n * 8 : (n + 1) * 8]
    s.gz2_in[depth] = s.gz2[depth]
    start(gz2_copy)
    one_lane = lax.broadcasted_iota(jnp.int32, (1, LANES), 1)
    row_term = jnp.where((one_lane >> 3) == plane, 0.5 * jnp.log(row_sum), 0.0)
    col_term = jnp.where((one_lane >> 3) == depth, 0.5 * jnp.log(col_sum), 0.0)
    loss_terms = row_term + col_term - score

    wait(s.unit_in.at[pl.ds(0, 15)], UNIT)
    grad_unit = s.unit_in[0]
    for n in range(1, SIDE):
        grad_unit = grad_unit + s.unit_in[n]
    dot = jnp.sum(z3 * grad_unit, axis=1, keepdims=True)
    grad_z3 = inverse * (grad_unit - z3 * dot * (inverse * inverse))

    ways = ((along_x, x_at, along_y, y_at), (along_y, y_at, along_x, x_at))

    def lanes_of(c, h):
        return pl.ds(CHUNKS[c][h][0], CHUNKS[c][h][1] - CHUNKS[c][h][0])

    def whole(c):
        return pl.ds(CHUNKS[c][0][0], CHUNKS[c][1][1] - CHUNKS[c][0][0])

    def core_copy(c):
        theirs = s.payload.at[pl.ds((1 - core) * 256, 256), whole(c)]
        return remote(theirs, s.core_in.at[:, whole(c)], sems, CORE + c, sibling)

    def first_copy(c, h, o):
        peer, lanes = ways[h][0][o], lanes_of(c, h)
        return remote(
            s.first_out.at[pl.ds(peer[2] * 64, 64), lanes],
            s.first_in.at[ways[h][1], :, lanes],
            sems,
            FIRST + 2 * c + h,
            peer[:2],
        )

    def second_copy(c, h, o):
        peer, lanes = ways[h][2][o], lanes_of(c, h)
        return remote(
            s.second_out.at[pl.ds(peer[2] * 16, 16), lanes],
            s.second_in.at[ways[h][3], :, lanes],
            sems,
            SECOND + 2 * c + h,
            peer[:2],
        )

    def ring_copy(c, h, o):
        lanes = lanes_of(c, h)
        return remote(
            s.ring_out.at[:, lanes],
            s.ring_in.at[ring, :, lanes],
            sems,
            RING + 2 * c + h,
            along_ring[o][:2],
        )

    def second_share(c, h, o):
        mine = summed.at[pl.ds(core * 256 + ways[h][1] * 64 + ways[h][3] * 16, 16), lanes_of(c, h)]
        return remote(mine, mine, sems, SHARE_SECOND + 2 * c + h, ways[h][2][o][:2])

    def first_share(c, h, o):
        mine = summed.at[pl.ds(core * 256 + ways[h][1] * 64, 64), lanes_of(c, h)]
        return remote(mine, mine, sems, SHARE_FIRST + 2 * c + h, ways[h][0][o][:2])

    def core_share(c, h):
        mine = summed.at[pl.ds(core * 256, 256), lanes_of(c, h)]
        return remote(mine, mine, sems, CORE_OUT + 2 * c + h, sibling)

    near, far = range(1, 4), range(1, DEPTH)

    def all_first(c, h):
        return all_of(s.first_in.at[pl.ds(0, 3), :, lanes_of(c, h)], FIRST + 2 * c + h)

    def all_second(c, h):
        return all_of(s.second_in.at[pl.ds(0, 3), :, lanes_of(c, h)], SECOND + 2 * c + h)

    def all_ring(c, h):
        return all_of(s.ring_in.at[pl.ds(0, 7), :, lanes_of(c, h)], RING + 2 * c + h)

    def all_second_share(c, h):
        return all_of(s.second_in.at[pl.ds(0, 3), :, lanes_of(c, h)], SHARE_SECOND + 2 * c + h)

    def all_first_share(c, h):
        return all_of(s.first_in.at[pl.ds(0, 3), :, lanes_of(c, h)], SHARE_FIRST + 2 * c + h)

    def added(ref, count, lanes):
        total = ref[0, :, lanes].astype(F32)
        for n in range(1, count):
            total = total + ref[n, :, lanes].astype(F32)
        return total.astype(BF)

    def first_step(c):
        core_copy(c).wait_recv()
        mine = s.payload[pl.ds(core * 256, 256), whole(c)].astype(F32)
        s.first_out[:, whole(c)] = (mine + s.core_in[:, whole(c)].astype(F32)).astype(BF)
        for h in range(2):
            for o in near:
                first_copy(c, h, o).start()
        for h in range(2):
            lanes, at = lanes_of(c, h), ways[h][1]
            s.first_in[at, :, lanes] = s.first_out[pl.ds(at * 64, 64), lanes]

    def second_step(c):
        for h in range(2):
            lanes, at = lanes_of(c, h), ways[h][3]
            all_first(c, h).wait_recv()
            s.second_out[:, lanes] = added(s.first_in, 4, lanes)
            for o in near:
                second_copy(c, h, o).start()
            s.second_in[at, :, lanes] = s.second_out[pl.ds(at * 16, 16), lanes]

    def ring_step(c):
        for h in range(2):
            lanes = lanes_of(c, h)
            all_second(c, h).wait_recv()
            total = added(s.second_in, 4, lanes)
            s.ring_out[:, lanes] = total
            for o in far:
                ring_copy(c, h, o).start()
            s.ring_in[ring, :, lanes] = total

    def share_second_step(c):
        for h in range(2):
            lanes = lanes_of(c, h)
            all_ring(c, h).wait_recv()
            at = pl.ds(core * 256 + ways[h][1] * 64 + ways[h][3] * 16, 16)
            summed[at, lanes] = added(s.ring_in, DEPTH, lanes)
            for o in near:
                second_share(c, h, o).start()

    def share_first_step(c):
        for h in range(2):
            all_second_share(c, h).wait_recv()
            for o in near:
                first_share(c, h, o).start()

    def share_core_step(c):
        for h in range(2):
            all_first_share(c, h).wait_recv()
            core_share(c, h).start()

    def arrive_step(c):
        for h in range(2):
            core_share(c, h).wait_recv()

    start_backward(grad_z3, wout, proj, s)
    value_backward(s)
    project_backward(s.dv, 2, VALUE, s)
    core_copy(0).start()
    attend_backward(0, 2, s)
    first_step(0)
    attend_backward(2, PAIRS, s)
    project_backward(s.dqs, 0, QUERY, s)
    core_copy(1).start()
    project_backward(s.dks, 1, KEY, s)
    first_step(1)
    bias_backward(s)
    gain_backward(wqkv, s)
    s.small[68:69, :] = loss_terms
    s.payload[:, SMALL:PAYLOAD] = s.small[...].astype(BF)
    core_copy(2).start()
    second_step(0)
    first_step(2)
    ring_step(0)
    second_step(1)
    second_step(2)
    ring_step(1)
    ring_step(2)
    share_second_step(0)
    share_first_step(0)
    share_second_step(1)
    share_second_step(2)
    share_first_step(1)
    share_core_step(0)
    share_first_step(2)
    share_core_step(1)
    arrive_step(0)
    qkv[:, 2 * WIDTH : 3 * WIDTH] = summed[:, VALUE:CTX].astype(F32)
    out[...] = mm_t(summed[:, CTX:HEAD], proj[...])
    head[...] = summed[:, HEAD:QUERY].astype(F32)
    share_core_step(2)
    arrive_step(1)
    qkv[:, 0:WIDTH] = summed[:, QUERY:KEY].astype(F32)

    wait(s.gz2_in.at[pl.ds(0, 15)], GZ2)
    total = s.gz2_in[0]
    for n in range(1, SIDE):
        total = total + s.gz2_in[n]
    grad_z2[...] = total
    arrive_step(2)
    qkv[:, WIDTH : 2 * WIDTH] = summed[:, KEY:SMALL].astype(F32)
    small[...] = summed[0:80, SMALL:PAYLOAD].astype(F32)
    for c in range(3):
        core_copy(c).wait_send()
        for h in range(2):
            for group in (all_first, all_second, all_ring, all_second_share, all_first_share):
                group(c, h).wait_send()
            core_share(c, h).wait_send()


SHAPES = {
    "xhat": ((256, WIDTH), F32),
    "normed": ((256, WIDTH), BF),
    "xsum": ((MOLS, WIDTH), F32),
    "perm": ((WIDTH, WIDE), BF),
    "q": ((PAIRS, ATOMS, WIDE), F32),
    "k": ((PAIRS, ATOMS, WIDE), F32),
    "v": ((PAIRS, ATOMS, WIDE), F32),
    "distance": ((MOLS, 1, ATOMS * ATOMS), F32),
    "bias_lhs": ((2 * LANES, 2 * KERNELS), BF),
    "basis": ((PAIRS, 2 * KERNELS, ATOMS * ATOMS), BF),
    "attn": ((PAIRS, ATOMS * ATOMS, LANES), F32),
    "column": ((PAIRS, ATOMS, LANES), F32),
    "bias_sum": ((2 * KERNELS, LANES), F32),
    "context": ((MOLS, 1, WIDE), F32),
    "ctx_sum": ((MOLS, WIDTH), F32),
    "pooled": ((MOLS, WIDTH), F32),
    "along": ((PAIRS, ATOMS, LANES), F32),
    "dk": ((ATOMS, WIDE), F32),
    "dqs": ((PAIRS, ATOMS, WIDE), BF),
    "dks": ((PAIRS, ATOMS, WIDE), BF),
    "dv": ((PAIRS, ATOMS, WIDE), BF),
    "dproj": ((256, 3 * WIDTH), BF),
    "small": ((WIDTH, LANES), F32),
    "payload": ((WIDTH, PAYLOAD), BF),
    "z2": ((LANES, LANES), F32),
    "pos": ((LANES, LANES), jnp.int32),
    "z3": ((LANES, LANES), F32),
    "rows": ((SIDE, 1, LANES), F32),
    "cols": ((SIDE, 1, LANES), F32),
    "unit": ((SIDE, 8, LANES), F32),
    "unit_in": ((SIDE, 8, LANES), F32),
    "gz2": ((SIDE, 8, LANES), F32),
    "gz2_in": ((SIDE, 8, LANES), F32),
    "core_in": ((256, PAYLOAD), BF),
    "first_out": ((256, PAYLOAD), BF),
    "first_in": ((4, 64, PAYLOAD), BF),
    "second_out": ((64, PAYLOAD), BF),
    "second_in": ((4, 16, PAYLOAD), BF),
    "ring_out": ((16, PAYLOAD), BF),
    "ring_in": ((DEPTH, 16, PAYLOAD), BF),
    "feats": ((256, WIDTH), BF),
    "wqkv": ((WIDTH, 3 * WIDTH), BF),
    "wout": ((WIDTH, WIDTH), BF),
    "proj": ((WIDTH, LANES), BF),
    "summed": ((WIDTH, PAYLOAD), BF),
}


class Scratch:
    def __init__(self, refs):
        for name, ref in zip(list(SHAPES) + ["send", "recv", "load"], refs):
            setattr(self, name, ref)


def unpack(
    qkv, out, head, small, cols_in, loss, cols_out, g_qkv, g_out, g_proj, g_bias, g_gain, sems
):
    copies = []

    def store(src, dst):
        copies.append(pltpu.make_async_copy(src, dst, sems.at[len(copies)]))
        copies[-1].start()

    for n in range(4):
        store(qkv.at[pl.ds(n * 128, 128), :], g_qkv.at[pl.ds(n * 128, 128), :])
    for n in range(2):
        store(out.at[pl.ds(n * 256, 256), :], g_out.at[pl.ds(n * 256, 256), :])
    store(head, g_proj)
    cols_out[...] = cols_in[...]
    g_bias[...] = small[0:64, :]
    for n in range(4):
        g_gain[:, n * LANES : (n + 1) * LANES] = small[64 + n : 65 + n, :]
    loss[...] = jnp.sum(small[68:69, :], axis=1, keepdims=True) / BATCH
    for copy in copies:
        copy.wait()


def on_device(
    atom_feats, coords, atom_counts, positives, z2, w_qkv, w_out, proj, bias_weight, ln_gain
):
    vmem = pl.BlockSpec(memory_space=pltpu.VMEM)
    smem = pl.BlockSpec(memory_space=pltpu.SMEM)
    hbm = pl.BlockSpec(memory_space=pl.ANY)
    left = pl.pallas_call(
        fused,
        out_shape=(
            pltpu.VMEM((WIDTH, 3 * WIDTH), F32),
            pltpu.VMEM((WIDTH, WIDTH), F32),
            pltpu.VMEM((WIDTH, LANES), F32),
            pltpu.VMEM((80, LANES), F32),
            pltpu.VMEM((8, LANES), F32),
        ),
        in_specs=[smem, smem, hbm, vmem, vmem, hbm, hbm, hbm, vmem, vmem],
        out_specs=(vmem,) * 5,
        scratch_shapes=[pltpu.VMEM(*shape) for shape in SHAPES.values()]
        + [pltpu.SemaphoreType.DMA((KINDS,))] * 2
        + [pltpu.SemaphoreType.DMA((4,))],
        compiler_params=pltpu.CompilerParams(
            collective_id=0, has_side_effects=True, vmem_limit_bytes=56 * 1024 * 1024
        ),
        name="pretrain_step",
    )(
        atom_counts,
        positives,
        atom_feats.reshape(256, WIDTH),
        coords.transpose(1, 0, 2),
        z2,
        w_qkv,
        w_out,
        proj,
        bias_weight.T,
        ln_gain.reshape(1, WIDTH),
    )
    shapes = ((1, 1), (8, LANES), (WIDTH, 3 * WIDTH), (WIDTH, WIDTH), (WIDTH, LANES), (HEADS, KERNELS), (1, WIDTH))
    loss, grad_z2, g_qkv, g_out, g_proj, g_bias, g_gain = pl.pallas_call(
        unpack,
        out_shape=tuple(jax.ShapeDtypeStruct(shape, F32) for shape in shapes),
        in_specs=[vmem] * 5,
        out_specs=(vmem, vmem, hbm, hbm, hbm, vmem, vmem),
        scratch_shapes=[pltpu.SemaphoreType.DMA((7,))],
        compiler_params=pltpu.CompilerParams(vmem_limit_bytes=32 * 1024 * 1024),
        name="unpack",
    )(*left)
    return (loss.reshape(()), grad_z2, g_qkv, g_out, g_proj, g_bias.T, g_gain.reshape(WIDTH))


def solution(mesh):
    return jax.shard_map(
        on_device,
        mesh=mesh,
        in_specs=(
            P(("dp", "group"), None, None),
            P(("dp", "group"), None, None),
            P(("dp", "group")),
            P(("dp", "group")),
            P(("dp", "group"), None),
            P(),
            P(),
            P(),
            P(),
            P(),
        ),
        out_specs=(P(), P(("dp", "group"), None), P(), P(), P(), P(), P()),
        check_vma=False,
    )
```
